32 devices in a mesh: group: 2 (over y), expert: 4 (over z), cuts: 4 (over x, core).
Axes of the slice: x: 2, y: 2, z: 4, core: 2. Of those that a mesh axis runs over, the one named last changes fastest.
Arguments:
- residual: bfloat16 [128, 7168], P(('group', 'expert', 'cuts')), parts along dimension 0, may hold values from -6 to 6
- head_partials: float32 [4, 128, 7168], P('cuts', ('group', 'expert')), parts along dimension 1, may hold values from -6 to 6
- norm_gain: float32 [7168], replicated, may hold values from 0.1 to 1.9
- routes: int32 [128, 8], P(('group', 'expert', 'cuts')), parts along dimension 0, may hold values from 0 to 15, all different within a row; in each aligned block of 4 rows (0 to 3, 4 to 7, ...) at most 3 rows name the same one
- route_weights: float32 [128, 8], P(('group', 'expert', 'cuts')), parts along dimension 0, may hold values from 0.1 to 1
- w_gate: bfloat16 [7168, 16384], P('cuts', 'expert'), may hold values from -0.0625 to 0.0625
- w_up: bfloat16 [7168, 16384], P('cuts', 'expert'), may hold values from -0.0625 to 0.0625
- w_down: bfloat16 [16384, 7168], P('expert', 'cuts'), may hold values from -0.1875 to 0.1875
- expert_scale: float32 [16], replicated, may hold values from 0.5 to 2
Outputs:
- mixed: bfloat16 [128, 7168], P(('group', 'expert', 'cuts')), parts along dimension 0
The draws below stay inside these ranges and needn't reach their ends.
There are 2 independent parts, one for each index of `group`. The reference program is written for one: setup_inputs(seed, part) draws one part's arguments, and reference() takes and returns one part's arrays. A program takes and returns all parts, laid end to end along the dimension named above; an argument that names none is the same for every part. Nothing has to cross between parts.
Inputs may be any that keep to these rules, and one draw needn't show every extreme that they name: `routes`: each row names 8 different experts; among the 4 rows of one device no expert is named by more than 3 rows.
All inputs are finite; a program needn't handle non-finite values.
Results may differ from the reference program's by a relative error of at most 0.0073.
Values may be sent and summed in bfloat16 or wider, within the bound.
No kernel may reach another device: no remote copies, remote signals or barrier semaphores. Data moves between devices by JAX's collectives and lax.ppermute only.
A program may use at most 448 MiB of HBM per device.

```python
import math
import jax
import jax.numpy as jnp
import numpy as np
from jax import lax

D = 7168
FH = 1024
EXPERTS = 16
TOPK = 8
ROW_DEV = 4
MOST = 3
ROWS = 64
N_EXPERT = 4
N_CUTS = 4


def shard_levels(key, shape, cuts, low, largest):
    def one(position, shards_of):
        draws = jax.random.uniform(jax.random.fold_in(jax.random.fold_in(key, 6), position), (shards_of,), jnp.float32, low / len(cuts), largest / len(cuts))
        return jnp.repeat(jnp.exp(draws), shape[position] // shards_of).reshape((-1,) + (1,) * (len(shape) - position - 1))

    factor_of = one(*cuts[0])
    for cut in cuts[1:]:
        factor_of = factor_of * one(*cut)
    return factor_of


def shared_out(rng, own, number, rows, amount, top, limit, slope):
    ranking = jax.random.permutation(rng, amount)
    packed, ordinary = shares(amount, rows * top, limit, slope, True), shares(amount, rows * top, limit, slope, False)
    places = jnp.arange(amount)

    def named(lengths, rotation):
        used = int((lengths > 0).sum())
        fixed = max(1, used // 4)
        moved = fixed + (places - fixed + rotation * (used - fixed)) % max(1, amount - fixed)
        return jnp.zeros((amount,), jnp.int32).at[ranking[jnp.where(places < fixed, places, moved)]].set(jnp.asarray(lengths, jnp.int32))

    lengths = jnp.where(number % 4 == 0, named(packed, number // 4), named(ordinary, number - number // 4 - 1))
    mixed = jax.random.permutation(jax.random.fold_in(own, 3), amount)
    donor, receiver = mixed[0:amount // 2 * 2:2], mixed[1:amount // 2 * 2:2]
    slack = jnp.minimum(lengths[donor] - 1, limit - lengths[receiver]) // 2
    slack = jnp.where((donor == ranking[0]) | (receiver == ranking[0]) | (lengths[receiver] == 0), 0, jnp.maximum(slack, 0))
    moved = jax.random.randint(jax.random.fold_in(own, 4), (amount // 2,), 0, 1 << 20) % (slack + 1)
    lengths = lengths.at[donor].add(-moved).at[receiver].add(moved)
    members = jnp.searchsorted(jnp.cumsum(lengths), jnp.arange(rows * top), side="right").astype(jnp.int32)
    table = members.reshape(top, rows).T
    table = table[jax.random.permutation(jax.random.fold_in(own, 1), rows)]
    rotation = jax.random.randint(jax.random.fold_in(own, 2), (rows, 1), 0, top)
    return jnp.take_along_axis(table, (jnp.arange(top)[None, :] + rotation) % top, axis=1)


def shares(number_of, total, most, slope, full):
    weights = [(1 << 20) // math.isqrt(standing ** slope) + 1 for standing in range(1, number_of + 1)]
    largest = most if full else min(most, max(-(-total // number_of), total * weights[0] // sum(weights)))
    least = 1 if total - largest >= number_of - 1 else 0
    given, surplus = [largest] + [least] * (number_of - 1), total - largest - least * (number_of - 1)
    while surplus > 0:
        free = [i for i in range(1, number_of) if given[i] < largest] or [i for i in range(1, number_of) if given[i] < most]
        mass, left = sum([weights[i] for i in free]), surplus
        for i in free:
            more = min(most - given[i], max(1, left * weights[i] // mass), surplus)
            given[i] = given[i] + more
            surplus = surplus - more
    return np.array(given)


def scatter_about(stream_key, dims, deviation, reach, cuts=(), kind=jnp.bfloat16):
    level = shard_levels(stream_key, dims, cuts, -0.22, 0.18) if cuts else 1.0
    values = jax.random.normal(stream_key, dims, jnp.float32) * deviation * level
    return jnp.minimum(jnp.maximum(values, -reach), reach).astype(kind)


def setup_inputs(seed: int = 0, part: int = 0) -> dict:
    streams_of = jax.random.split(jax.random.key(seed), 10)
    own_keys = jax.random.split(jax.random.fold_in(streams_of[9], part), 10)
    residual = scatter_about(own_keys[0], (ROWS, D), 1.0, 6.0, ((0, 16),))
    head_partials = scatter_about(own_keys[1], (N_CUTS, ROWS, D), 0.5, 6.0, ((0, 4), (1, 4)), jnp.float32)
    norm_gain = jnp.clip(1.0 + 0.18 * jax.random.normal(streams_of[2], (D,), jnp.float32), 0.1, 1.9)
    routes_keys = jax.random.split(jax.random.fold_in(own_keys[3], 1), ROWS // ROW_DEV)
    routes_turns = jax.random.permutation(jax.random.fold_in(own_keys[3], 3), ROWS // ROW_DEV)
    routes = jax.vmap(lambda own, number: shared_out(jax.random.fold_in(own_keys[3], 2), own, number, ROW_DEV, EXPERTS, TOPK, MOST, 2))(routes_keys, routes_turns).reshape((ROWS, TOPK))
    route_weights = jnp.clip(0.1 + 0.9 * jax.random.uniform(own_keys[4], (ROWS, TOPK), jnp.float32) ** shard_levels(own_keys[4], (ROWS, TOPK), ((0, 16),), -0.2, 0.2), 0.1, 1.0)
    w_gate = scatter_about(streams_of[5], (D, EXPERTS * FH), D ** -0.5, 0.0625, ((0, 4), (1, 4)))
    w_up = scatter_about(streams_of[6], (D, EXPERTS * FH), D ** -0.5, 0.0625, ((0, 4), (1, 4)))
    w_down = scatter_about(streams_of[7], (EXPERTS * FH, D), FH ** -0.5, 0.1875, ((0, 4), (1, 4)))
    expert_scale = jnp.clip(jnp.exp(jax.random.uniform(streams_of[8], (EXPERTS,), jnp.float32, math.log(0.5), math.log(2.0))), 0.5, 2.0)
    return {"residual": residual, "head_partials": head_partials, "norm_gain": norm_gain, "routes": routes, "route_weights": route_weights, "w_gate": w_gate, "w_up": w_up, "w_down": w_down, "expert_scale": expert_scale}


def reference(residual, head_partials, norm_gain, routes, route_weights, w_gate, w_up, w_down, expert_scale):
    attention = lax.optimization_barrier(jnp.sum(head_partials, 0))
    stream_half = lax.optimization_barrier((residual.astype(jnp.float32) + attention).astype(jnp.bfloat16))
    stream = stream_half.astype(jnp.float32)
    mean_square = lax.optimization_barrier(jnp.mean(stream * stream, 1, keepdims=True))
    normed = (stream * lax.rsqrt(mean_square + 1e-06) * norm_gain).astype(jnp.bfloat16)
    block_width = EXPERTS * FH // N_EXPERT
    piece_width = min(FH, block_width)
    piece_count = FH // piece_width

    def one_expert(totals, expert):
        start = expert * FH
        gate_cols = lax.dynamic_slice_in_dim(w_gate, start, FH, 1)
        up_cols = lax.dynamic_slice_in_dim(w_up, start, FH, 1)
        down_rows = lax.dynamic_slice_in_dim(w_down, start, FH, 0)
        gate = jnp.dot(normed, gate_cols, preferred_element_type=jnp.float32)
        upper = jnp.dot(normed, up_cols, preferred_element_type=jnp.float32)
        hidden = (jax.nn.silu(gate) * upper * expert_scale[expert]).astype(jnp.bfloat16)
        pieces = jnp.einsum('rpk,pkd->rpd', hidden.reshape(ROWS, piece_count, piece_width).astype(jnp.float32), down_rows.reshape(piece_count, piece_width, D).astype(jnp.float32))
        rounded = lax.optimization_barrier(pieces.astype(jnp.bfloat16)).astype(jnp.float32)
        partial_value = lax.optimization_barrier(jnp.sum(rounded, 1))
        share = lax.optimization_barrier(jnp.sum(jnp.where(routes == expert, route_weights, 0.0), 1))
        return (totals + share[:, None] * partial_value, None)
    expert_sum, unused = lax.scan(one_expert, jnp.zeros((ROWS, D), jnp.float32), jnp.arange(EXPERTS, dtype=jnp.int32))
    return (stream + expert_sum).astype(jnp.bfloat16)
```

```python
import jax
import jax.numpy as jnp
from jax import lax
from jax.sharding import PartitionSpec as P

FH = 1024
EXPERTS = 16
bf16, f32 = jnp.bfloat16, jnp.float32


def shift(x, axis, k):
    n = lax.axis_size(axis)
    return lax.ppermute(x, axis, [(i, (i + k) % n) for i in range(n)])


def swap(x, axis, bit):
    n = lax.axis_size(axis)
    return lax.ppermute(x, axis, [(i, i ^ bit) for i in range(n)])


def pick(x, i):
    return lax.dynamic_index_in_dim(x, i, 0, False)


def body(
    residual, head_partials, norm_gain, routes, route_weights, w_gate, w_up, w_down, expert_scale
):
    n_e, n_c = lax.axis_size("expert"), lax.axis_size("cuts")
    e, c = lax.axis_index("expert"), lax.axis_index("cuts")
    own_rows, width = residual.shape
    rows_e = own_rows * n_c
    part = width // n_c
    block = w_gate.shape[1]
    rows = rows_e * n_e
    b, h = c & 1, c >> 1

    share = jnp.sum(
        jnp.where(
            routes[:, :, None] == jnp.arange(EXPERTS, dtype=jnp.int32), route_weights[:, :, None], 0.0
        ),
        1,
    )
    share = lax.all_gather(share, ("expert", "cuts"), axis=0, tiled=True)

    y = head_partials.reshape(rows_e, width)
    mine = lax.dynamic_slice_in_dim(y, c * own_rows, own_rows, 0) + residual.astype(f32)
    y = lax.dynamic_update_slice_in_dim(y, mine, c * own_rows, 0)
    y = y.reshape(rows_e, n_c // 2, 2, part).transpose(2, 1, 0, 3)
    y = pick(y, b) + swap(pick(y, 1 - b), "cuts", 1)
    y = pick(y, h) + swap(pick(y, 1 - h), "cuts", 2)
    own_stream = y.astype(bf16)

    if n_e <= 8:
        pieces = [own_stream] + [shift(own_stream, "expert", k) for k in range(1, n_e)]
        stacked = jnp.stack(pieces)
        order = (e - jnp.arange(n_e)) % n_e
        stream = jnp.take(stacked, order, axis=0).reshape(rows, part)
    else:
        stream = lax.all_gather(own_stream, "expert", axis=0, tiled=True)
    sf = stream.astype(f32)
    square = jnp.sum(sf * sf, 1, keepdims=True)
    square = square + swap(square, "cuts", 1)
    square = square + swap(square, "cuts", 2)
    factor = lax.rsqrt(square / width + 1e-06)
    gain = lax.dynamic_slice_in_dim(norm_gain, c * part, part, 0)
    x = (sf * gain).astype(bf16)

    def product(w):
        p = jnp.dot(x, w, preferred_element_type=f32).astype(bf16)
        p = p.reshape(rows, n_c // 2, 2, block // n_c).transpose(2, 1, 0, 3)
        return p

    g, u = product(w_gate), product(w_up)
    p = jnp.stack([g, u], 2)
    p = pick(p, b).astype(f32) + swap(pick(p, 1 - b), "cuts", 1).astype(f32)
    keep, send = pick(p, h), pick(p, 1 - h).astype(bf16)
    p = keep + swap(send, "cuts", 2).astype(f32)
    g, u = p[0] * factor, p[1] * factor
    unit = e * block + (h * 2 + b) * (block // n_c) + jnp.arange(block // n_c, dtype=jnp.int32)
    coefficient = share * expert_scale
    coefficient = jnp.dot(
        coefficient,
        (jnp.arange(EXPERTS, dtype=jnp.int32)[:, None] == (unit // FH)[None, :]).astype(f32),
        precision=lax.Precision.HIGHEST,
    )
    hidden = (jax.nn.silu(g) * u * coefficient).astype(bf16)
    other = swap(hidden, "cuts", 2)
    pair = jnp.where(h == 0, jnp.stack([hidden, other]), jnp.stack([other, hidden]))
    other = swap(pair, "cuts", 1)
    quad = jnp.where(b == 0, jnp.stack([pair, other], 1), jnp.stack([other, pair], 1))
    hidden = quad.transpose(2, 0, 1, 3).reshape(rows, block)
    out = jnp.dot(hidden, w_down, preferred_element_type=f32)

    if n_e <= 8:
        out = out.reshape(n_e, rows_e, part)
        total = pick(out, e)
        for k in range(1, n_e):
            total = total + shift(pick(out, (e + k) % n_e).astype(bf16), "expert", k).astype(f32)
    else:
        total = lax.psum_scatter(out, "expert", scatter_dimension=0, tiled=True)
    mixed = (own_stream.astype(f32) + total).astype(bf16)
    mixed = lax.all_to_all(
        mixed.reshape(n_c, own_rows, part), "cuts", split_axis=0, concat_axis=0, tiled=True
    )
    return mixed.transpose(1, 0, 2).reshape(own_rows, width)


def solution(mesh):
    in_specs = (
        P(("group", "expert", "cuts"), None),
        P("cuts", ("group", "expert"), None),
        P(),
        P(("group", "expert", "cuts"), None),
        P(("group", "expert", "cuts"), None),
        P("cuts", "expert"),
        P("cuts", "expert"),
        P("expert", "cuts"),
        P(),
    )
    out_specs = P(("group", "expert", "cuts"), None)
    return jax.shard_map(body, mesh=mesh, in_specs=in_specs, out_specs=out_specs, check_vma=False)
```

```python
import functools

import jax
import jax.numpy as jnp
from jax import lax
from jax.experimental import pallas as pl
from jax.experimental.pallas import tpu as pltpu
from jax.sharding import PartitionSpec as P

FH = 1024
EXPERTS = 16
SPLIT = 4
MOST = 3
bf16, f32 = jnp.bfloat16, jnp.float32


def shift(x, axis, k):
    n = lax.axis_size(axis)
    return lax.ppermute(x, axis, [(i, (i + k) % n) for i in range(n)])


def swap(x, axis, bit):
    n = lax.axis_size(axis)
    return lax.ppermute(x, axis, [(i, i ^ bit) for i in range(n)])


def pick(x, i):
    return lax.dynamic_index_in_dim(x, i, 0, False)


def body(
    residual, head_partials, norm_gain, routes, route_weights, w_gate, w_up, w_down, expert_scale
):
    n_e, n_c = lax.axis_size("expert"), lax.axis_size("cuts")
    e, c = lax.axis_index("expert"), lax.axis_index("cuts")
    own_rows, width = residual.shape
    rows_e = own_rows * n_c
    part = width // n_c
    block = w_gate.shape[1]
    rows = rows_e * n_e
    b, h = c & 1, c >> 1

    share = jnp.sum(
        jnp.where(
            routes[:, :, None] == jnp.arange(EXPERTS, dtype=jnp.int32), route_weights[:, :, None], 0.0
        ),
        1,
    )
    share = lax.all_gather(share, ("expert", "cuts"), axis=0, tiled=True)

    y = head_partials.reshape(rows_e, width)
    mine = lax.dynamic_slice_in_dim(y, c * own_rows, own_rows, 0) + residual.astype(f32)
    y = lax.dynamic_update_slice_in_dim(y, mine, c * own_rows, 0)
    y = y.reshape(rows_e, n_c // 2, 2, part).transpose(2, 1, 0, 3)
    y = pick(y, b) + swap(pick(y, 1 - b), "cuts", 1)
    y = pick(y, h) + swap(pick(y, 1 - h), "cuts", 2)
    own_stream = y.astype(bf16)

    if n_e <= 8:
        pieces = [own_stream] + [shift(own_stream, "expert", k) for k in range(1, n_e)]
        stacked = jnp.stack(pieces)
        order = (e - jnp.arange(n_e)) % n_e
        stream = jnp.take(stacked, order, axis=0).reshape(rows, part)
    else:
        stream = lax.all_gather(own_stream, "expert", axis=0, tiled=True)
    sf = stream.astype(f32)
    square = jnp.sum(sf * sf, 1, keepdims=True)
    square = square + swap(square, "cuts", 1)
    square = square + swap(square, "cuts", 2)
    factor = lax.rsqrt(square / width + 1e-06)
    gain = lax.dynamic_slice_in_dim(norm_gain, c * part, part, 0)
    x = (sf * gain).astype(bf16)

    def product(w):
        p = jnp.dot(x, w, preferred_element_type=f32).astype(bf16)
        p = p.reshape(rows, n_c // 2, 2, block // n_c).transpose(2, 1, 0, 3)
        return p

    g, u = product(w_gate), product(w_up)
    p = jnp.stack([g, u], 2)
    p = pick(p, b).astype(f32) + swap(pick(p, 1 - b), "cuts", 1).astype(f32)
    keep, send = pick(p, h), pick(p, 1 - h).astype(bf16)
    p = keep + swap(send, "cuts", 2).astype(f32)
    g, u = p[0] * factor, p[1] * factor
    unit = e * block + (h * 2 + b) * (block // n_c) + jnp.arange(block // n_c, dtype=jnp.int32)
    coefficient = share * expert_scale
    coefficient = jnp.dot(
        coefficient,
        (jnp.arange(EXPERTS, dtype=jnp.int32)[:, None] == (unit // FH)[None, :]).astype(f32),
        precision=lax.Precision.HIGHEST,
    )
    hidden = (jax.nn.silu(g) * u * coefficient).astype(bf16)
    other = swap(hidden, "cuts", 2)
    pair = jnp.where(h == 0, jnp.stack([hidden, other]), jnp.stack([other, hidden]))
    other = swap(pair, "cuts", 1)
    quad = jnp.where(b == 0, jnp.stack([pair, other], 1), jnp.stack([other, pair], 1))
    hidden = quad.transpose(2, 0, 1, 3).reshape(rows, block)
    out = jnp.dot(hidden, w_down, preferred_element_type=f32)

    if n_e <= 8:
        out = out.reshape(n_e, rows_e, part)
        total = pick(out, e)
        for k in range(1, n_e):
            total = total + shift(pick(out, (e + k) % n_e).astype(bf16), "expert", k).astype(f32)
    else:
        total = lax.psum_scatter(out, "expert", scatter_dimension=0, tiled=True)
    mixed = (own_stream.astype(f32) + total).astype(bf16)
    mixed = lax.all_to_all(
        mixed.reshape(n_c, own_rows, part), "cuts", split_axis=0, concat_axis=0, tiled=True
    )
    return mixed.transpose(1, 0, 2).reshape(own_rows, width)


MIB = 1 << 20
VM = pl.BlockSpec(memory_space=pltpu.VMEM)
PAD = 128
QUICK = pl.CostEstimate(flops=1, bytes_accessed=1, transcendentals=0)


HB = pl.BlockSpec(memory_space=pltpu.HBM)


def call(kernel, outs, *args, limit=4, scratch=(), far=0, inside=False):
    return pl.pallas_call(
        kernel,
        in_specs=[VM] * (len(args) - far) + [HB] * far,
        out_specs=[VM] * len(outs),
        out_shape=[pltpu.VMEM(*o) for o in outs] if inside else [jax.ShapeDtypeStruct(*o) for o in outs],
        scratch_shapes=list(scratch),
        cost_estimate=QUICK,
        compiler_params=pltpu.CompilerParams(vmem_limit_bytes=limit * MIB),
    )(*args)


def halves(v):
    high = v.astype(bf16)
    return high, (v - high.astype(f32)).astype(bf16)


def column(table, i):
    lane = lax.broadcasted_iota(jnp.int32, table.shape, 1)
    return jnp.sum(jnp.where(lane == i, table, 0.0), 1, keepdims=True)


def split_kernel(*refs):
    inputs, outs, scratch, sem = refs[:6], refs[6:10], refs[10:16], refs[16]
    heads, residual, routes, weights, gains, scales = scratch
    send, keep, gain, scale = outs
    copies = [
        pltpu.make_async_copy(a.at[0] if i == 0 else a, t, sem.at[i])
        for i, (a, t) in enumerate(zip(inputs, scratch))
    ]
    for copy in copies:
        copy.start()
    for copy in copies:
        copy.wait()
    c = lax.axis_index("cuts")
    b = c & 1
    rows, width = heads.shape
    own = residual.shape[0]
    n_c = rows // own
    part = width // n_c
    at = lax.broadcasted_iota(jnp.int32, (rows, 1), 0) // own == c

    def wide(v):
        return jnp.where(at, jnp.concatenate([v] * n_c, 0), 0.0)

    for x in range(n_c // 2):
        low = pl.ds(2 * x * part, part)
        high = pl.ds((2 * x + 1) * part, part)
        v0 = heads[:, low] + wide(residual[:, low].astype(f32))
        v1 = heads[:, high] + wide(residual[:, high].astype(f32))
        to = pl.ds(x * part, part)
        keep[:, to] = jnp.where(b == 0, v0, v1)
        send[:, to] = jnp.where(b == 0, v1, v0)
    lane = lax.broadcasted_iota(jnp.int32, (own, PAD), 1)
    share = jnp.zeros((own, PAD), f32)
    for k in range(routes.shape[1]):
        share = share + jnp.where(lane == routes[:, k : k + 1], weights[:, k : k + 1], 0.0)
    share = wide(share)
    end = pl.ds(n_c // 2 * part, PAD)
    keep[:, end] = share
    send[:, end] = share
    scale[...] = scales[...]
    lines = part // PAD
    for i in range(lines):
        gain[:, i * PAD : (i + 1) * PAD] = gains[pl.ds(c * lines + i, 1), :]


def join_kernel(keep, got, send, left):
    h = lax.axis_index("cuts") >> 1
    part = left.shape[1] - PAD
    v0 = keep[:, :part] + got[:, :part]
    v1 = keep[:, part : 2 * part] + got[:, part : 2 * part]
    share = keep[:, 2 * part :] + got[:, 2 * part :]
    left[:, :part] = jnp.where(h == 0, v0, v1)
    send[:, :part] = jnp.where(h == 0, v1, v0)
    left[:, part:] = share
    send[:, part:] = share


def stream_kernel(left, got, gate, up, out, gate_out, up_out):
    part = left.shape[1] - PAD
    out[:, :part] = (left[:, :part] + got[:, :part]).astype(bf16)
    high, low = halves(left[:, part:] + got[:, part:])
    lane = lax.broadcasted_iota(jnp.int32, high.shape, 1)
    low = pltpu.roll(jnp.where(lane < EXPERTS, low.astype(f32), 0.0), EXPERTS, 1)
    out[:, part:] = (jnp.where(lane < EXPERTS, high.astype(f32), 0.0) + low).astype(bf16)


def load_experts(experts, w_gate, w_up, outs, sem):
    copies = []
    for k, expert in enumerate(experts):
        for w, out in ((w_gate, outs[2 * k]), (w_up, outs[2 * k + 1])):
            at = pl.ds(pl.multiple_of(expert * FH, FH), FH)
            n = len(copies)
            step = w.shape[0] // SPLIT
            for p in range(SPLIT):
                rows = pl.ds(p * step, step)
                copies.append(pltpu.make_async_copy(w.at[rows, at], out.at[rows], sem.at[n + p]))
    for copy in copies:
        copy.start()
    return copies


def expert_of(pair, other):
    b = lax.axis_index("cuts") & 1
    return 2 * pair + (1 - b if other else b)


def loads(which, part, after, w_gate, w_up, limit, held=()):
    n, h = 2 * len(which), len(held)

    def kernel(*refs):
        sem = refs[-1]
        copies = load_experts(
            [expert_of(*w) for w in which], refs[h + 1], refs[h + 2], refs[2 * h + 3 : -1], sem
        )
        for copy in copies:
            copy.wait()

    return pl.pallas_call(
        kernel,
        in_specs=[VM] * h + [HB] * 3,
        out_specs=[VM] * (h + n),
        out_shape=[pltpu.VMEM((part, FH), bf16)] * (h + n),
        input_output_aliases={i: i for i in range(h)},
        scratch_shapes=[pltpu.SemaphoreType.DMA((SPLIT * n,))],
        cost_estimate=QUICK,
        compiler_params=pltpu.CompilerParams(vmem_limit_bytes=limit * MIB),
    )(*held, after, w_gate, w_up)


def load_down_kernel(after, w_down, *refs):
    outs, token, sem = refs[:-2], refs[-2], refs[-1]
    copies = []
    for i, (pair, other) in enumerate(((0, False), (0, True), (1, False), (1, True))):
        at = pl.ds(pl.multiple_of(expert_of(pair, other) * FH, FH), FH)
        copies.append(pltpu.make_async_copy(w_down.at[at], outs[i], sem.at[i]))
    for copy in copies:
        copy.start()
    for copy in copies:
        copy.wait()
    token[...] = jnp.zeros_like(token)


def expert_product(x, w_gate, w_up, out):
    tile = 256
    for w, base in ((w_gate, 0), (w_up, FH)):
        for i in range(FH // tile):
            p = jnp.dot(x[...], w[:, i * tile : (i + 1) * tile], preferred_element_type=f32)
            out[:, pl.ds(base + i * tile, tile)] = p.astype(out.dtype)


def first_kernel(s0, s1, s2, s3, gain, w_gate, w_up, x, send, share, square):
    part = x.shape[1]
    rows_e = s0.shape[0]
    weight = gain[...]
    for k, s in enumerate((s0, s1, s2, s3)):
        v = s[:, :part].astype(f32)
        at = pl.ds(k * rows_e, rows_e)
        x[at, :] = (v * weight).astype(bf16)
        square[at, :] = jnp.broadcast_to(jnp.sum(v * v, 1, keepdims=True), (rows_e, PAD))
        t = s[:, part:].astype(f32)
        lane = lax.broadcasted_iota(jnp.int32, t.shape, 1)
        t = t + pltpu.roll(t, PAD - EXPERTS, 1)
        share[at, :] = jnp.where(lane < EXPERTS, t, 0.0)
    expert_product(x, w_gate, w_up, send)
    send[:, 2 * FH :] = parts(square[...])


def parts(v):
    high, low = halves(v)
    lane = lax.broadcasted_iota(jnp.int32, v.shape, 1)
    return jnp.where(lane == 0, high.astype(f32), low.astype(f32)).astype(bf16)


def pair_sum(t):
    lane = lax.broadcasted_iota(jnp.int32, t.shape, 1)
    return jnp.broadcast_to(jnp.sum(jnp.where(lane < 2, t, 0.0), 1, keepdims=True), t.shape)


def product_kernel(x, w_gate, w_up, out):
    expert_product(x, w_gate, w_up, out)


def product_stream_kernel(x, gate_hbm, up_hbm, out, gate, up, sem):
    expert = expert_of(1, False)
    at = pl.ds(pl.multiple_of(expert * FH, FH), FH)
    step = 256
    parts_of = x.shape[1] // step
    copies = []
    for p in range(parts_of):
        rows = pl.ds(p * step, step)
        for w, t in ((gate_hbm, gate), (up_hbm, up)):
            copies.append(pltpu.make_async_copy(w.at[rows, at], t.at[rows], sem.at[len(copies)]))
    for copy in copies:
        copy.start()
    for p in range(parts_of):
        rows = pl.ds(p * step, step)
        for k, t in enumerate((gate, up)):
            copies[2 * p + k].wait()
            v = jnp.dot(x[:, rows], t[rows, :], preferred_element_type=f32)
            to = pl.ds(k * FH, FH)
            out[:, to] = v if p == 0 else out[:, to] + v


def own_expert(pair):
    e = lax.axis_index("expert")
    return e * (EXPERTS // lax.axis_size("expert")) + expert_of(pair, False)


def places(share, own_rows, slots):
    rows = share.shape[0]
    on = jnp.where(share != 0.0, 1.0, 0.0)
    row = lax.broadcasted_iota(jnp.int32, (rows, 1), 0)
    within = row % own_rows
    before = jnp.zeros_like(on)
    wide = jnp.broadcast_to(on, (rows, PAD))
    for d in range(1, own_rows):
        before = before + jnp.where(within >= d, pltpu.roll(wide, d, 0)[:, :1], 0.0)
    slot = row // own_rows * MOST + before.astype(jnp.int32)
    at = lax.broadcasted_iota(jnp.int32, (rows, slots), 1)
    return jnp.where((at == slot) & (on != 0.0), 1.0, 0.0).astype(bf16)


def packed(v, where):
    dims = (((0,), (0,)), ((), ()))
    return lax.dot_general(where, v, dims, preferred_element_type=f32).astype(bf16)


def payload(v, square, share, pair, own_rows, send, place):
    where = places(column(share[...], own_expert(pair)), own_rows, send.shape[0])
    place[...] = where
    send[:, : 2 * FH] = packed(v.astype(bf16), where)
    send[:, 2 * FH :] = packed(parts(square), where)


def first_sum_kernel(own_rows, keep, got, square, share, total, send, square_out, place):
    v = keep[...] + got[:, : 2 * FH].astype(f32)
    total[...] = v
    s = square[...] + pair_sum(got[:, 2 * FH :].astype(f32))
    square_out[...] = s
    payload(v, s, share, 0, own_rows, send, place)


def sum_kernel(own_rows, keep, got, square, share, total, send, place):
    v = keep[...] + got[...].astype(f32)
    total[...] = v
    payload(v, square[...], share, 1, own_rows, send, place)


def hidden_kernel(pair, width, total, got, square, place, share, scale, after, out):
    squares = pair_sum(jnp.dot(place[...], got[:, 2 * FH :], preferred_element_type=f32))
    factor = lax.rsqrt((square[...] + squares) / width + 1e-06)[:, :1]
    expert = own_expert(pair)
    coefficient = column(share[...], expert) * column(scale[...], expert)
    v = jnp.dot(place[...], got[:, : 2 * FH], preferred_element_type=f32)
    v = (total[...] + v) * factor
    g, u = v[:, :FH], v[:, FH:]
    out[...] = (g / (1.0 + jnp.exp(-g)) * u * coefficient).astype(bf16)


def down_kernel(last, *refs):
    if last:
        hidden, w_down, before, o0, o1, o2, o3 = refs
    elif len(refs) == 4:
        hidden, w_down, before, out = refs
    else:
        (hidden, w_down, out), before = refs, None
    tile = 256
    for i in range(w_down.shape[1] // tile):
        cols = pl.ds(i * tile, tile)
        p = jnp.dot(hidden[...], w_down[:, cols], preferred_element_type=f32)
        if before is not None:
            p = p + before[:, cols]
        if last:
            r = o0.shape[0]
            for k, o in enumerate((o0, o1, o2, o3)):
                o[:, cols] = p[k * r : (k + 1) * r].astype(o.dtype)
        else:
            out[:, cols] = p


def mixed_kernel(stream, own, r1, r2, r3, m0, m1, m2, m3):
    c = lax.axis_index("cuts")
    part = own.shape[1]
    v = stream[:, :part].astype(f32) + own[...]
    for r in (r1, r2, r3):
        v = v + r[...].astype(f32)
    n = m0.shape[0]
    blocks = [v[k * n : (k + 1) * n] for k in range(4)]
    for k, m in enumerate((m0, m1, m2, m3)):
        to = c ^ k
        t = jnp.where(to < 2, jnp.where(to == 0, blocks[0], blocks[1]),
                      jnp.where(to == 2, blocks[2], blocks[3]))
        m[...] = t.astype(bf16)


def final_kernel(m0, m1, m2, m3, out):
    c = lax.axis_index("cuts")
    part = m0.shape[1]
    p = [m[...].astype(f32) for m in (m0, m1, m2, m3)]
    for s in range(4):
        k = c ^ s
        t = jnp.where(k < 2, jnp.where(k == 0, p[0], p[1]), jnp.where(k == 2, p[2], p[3]))
        out[:, s * part : (s + 1) * part] = t.astype(bf16)


def fast_body(
    residual, head_partials, norm_gain, routes, route_weights, w_gate, w_up, w_down, expert_scale
):
    own_rows, width = residual.shape
    rows_e = 4 * own_rows
    part = width // 4
    rows = 4 * rows_e
    slots = rows // own_rows * MOST
    weight = pltpu.VMEM((part, FH), bf16)

    cut = (rows_e, 2 * part + PAD)
    gains, scales = norm_gain.reshape(width // PAD, PAD), expert_scale.reshape(1, EXPERTS)
    send, keep, gain, scale = call(
        split_kernel, [(cut, f32)] * 2 + [((1, part), f32), ((1, EXPERTS), f32)],
        head_partials, residual, routes, route_weights, gains, scales,
        far=6, limit=62, inside=True,
        scratch=[
            pltpu.VMEM((rows_e, width), f32), pltpu.VMEM(residual.shape, bf16),
            pltpu.VMEM(routes.shape, jnp.int32), pltpu.VMEM(route_weights.shape, f32),
            pltpu.VMEM(gains.shape, f32), pltpu.VMEM(scales.shape, f32),
            pltpu.SemaphoreType.DMA((6,)),
        ],
    )
    cut = (rows_e, part + PAD)
    send, left = call(join_kernel, [(cut, f32)] * 2, keep, swap(send, "cuts", 1))
    got = swap(send, "cuts", 2)
    ga0, ua0 = loads([(0, True)], part, send, w_gate, w_up, 42)
    s0, ga0, ua0 = pl.pallas_call(
        stream_kernel,
        in_specs=[VM] * 4,
        out_specs=[VM] * 3,
        out_shape=[jax.ShapeDtypeStruct(cut, bf16), weight, weight],
        input_output_aliases={2: 1, 3: 2},
        cost_estimate=QUICK,
        compiler_params=pltpu.CompilerParams(vmem_limit_bytes=4 * MIB),
    )(left, got, ga0, ua0)
    s3, s2, s1 = [swap(s0, "expert", k) for k in (3, 2, 1)]
    ga0, ua0, gb0, ub0, ga1, ua1 = loads(
        [(0, False), (1, True)], part, s0, w_gate, w_up, 29, (ga0, ua0)
    )

    x, send, share, square = call(
        first_kernel,
        [((rows, part), bf16), ((rows, 2 * FH + PAD), bf16), ((rows, PAD), f32), ((rows, PAD), f32)],
        s0, s1, s2, s3, gain, ga0, ua0,
    )
    got = swap(send, "cuts", 1)
    full = ((rows, 2 * FH), f32)
    (keep,) = call(product_kernel, [full], x, gb0, ub0)
    table = ((rows, PAD), f32)
    sent_all = ((rows, 2 * FH), bf16)
    place = ((rows, slots), bf16)
    sent = ((slots, 2 * FH + PAD), bf16)
    total0, send, square, place0 = call(
        functools.partial(first_sum_kernel, own_rows),
        [full, sent, table, place], keep, got, square, share,
    )
    got0 = swap(send, "cuts", 2)
    (send,) = call(product_kernel, [sent_all], x, ga1, ua1)
    got = swap(send, "cuts", 1)
    (keep,) = call(
        product_stream_kernel, [full], x, w_gate, w_up, far=2, limit=40,
        scratch=[
            pltpu.VMEM((part, FH), bf16), pltpu.VMEM((part, FH), bf16),
            pltpu.SemaphoreType.DMA((2 * (part // 256),)),
        ],
    )
    total1, send, place1 = call(
        functools.partial(sum_kernel, own_rows), [full, sent, place], keep, got, square, share
    )
    got1 = swap(send, "cuts", 2)
    d0, d1, d2, d3, after = pl.pallas_call(
        load_down_kernel,
        in_specs=[HB] * 2,
        out_specs=[VM] * 5,
        out_shape=[pltpu.VMEM((FH, part), bf16)] * 4 + [jax.ShapeDtypeStruct((8, PAD), f32)],
        scratch_shapes=[pltpu.SemaphoreType.DMA((4,))],
        cost_estimate=QUICK,
        compiler_params=pltpu.CompilerParams(vmem_limit_bytes=34 * MIB),
    )(send, w_down)

    half = ((rows, FH), bf16)
    out = ((rows, part), f32)
    (h0,) = call(
        functools.partial(hidden_kernel, 0, width), [half],
        total0, got0, square, place0, share, scale, after,
    )
    g0 = swap(h0, "cuts", 1)
    (t,) = call(functools.partial(down_kernel, False), [out], h0, d0)
    (t,) = call(functools.partial(down_kernel, False), [out], g0, d1, t)
    (h1,) = call(
        functools.partial(hidden_kernel, 1, width), [half],
        total1, got1, square, place1, share, scale, after,
    )
    g1 = swap(h1, "cuts", 1)
    (t,) = call(functools.partial(down_kernel, False), [out], h1, d2, t)
    o0, o1, o2, o3 = call(
        functools.partial(down_kernel, True),
        [((rows_e, part), f32)] + [((rows_e, part), bf16)] * 3,
        g1, d3, t,
    )
    r3, r2, r1 = [swap(o, "expert", k) for k, o in ((3, o3), (2, o2), (1, o1))]
    m0, m1, m2, m3 = call(mixed_kernel, [((own_rows, part), bf16)] * 4, s0, o0, r1, r2, r3)
    m2, m3, m1 = [swap(m, "cuts", k) for k, m in ((2, m2), (3, m3), (1, m1))]
    (mixed,) = call(final_kernel, [((own_rows, width), bf16)], m0, m1, m2, m3)
    return mixed


def solution(mesh):
    in_specs = (
        P(("group", "expert", "cuts"), None),
        P("cuts", ("group", "expert"), None),
        P(),
        P(("group", "expert", "cuts"), None),
        P(("group", "expert", "cuts"), None),
        P("cuts", "expert"),
        P("cuts", "expert"),
        P("expert", "cuts"),
        P(),
    )
    out_specs = P(("group", "expert", "cuts"), None)
    small = mesh.shape["expert"] == 4 and mesh.shape["cuts"] == 4
    return jax.shard_map(
        fast_body if small else body, mesh=mesh, in_specs=in_specs, out_specs=out_specs, check_vma=False
    )
```

```python
import functools

import jax
import jax.numpy as jnp
from jax import lax
from jax.experimental import pallas as pl
from jax.experimental.pallas import tpu as pltpu
from jax.sharding import PartitionSpec as P

FH = 1024
EXPERTS = 16
SPLIT = 4
MOST = 3
bf16, f32 = jnp.bfloat16, jnp.float32


def shift(x, axis, k):
    n = lax.axis_size(axis)
    return lax.ppermute(x, axis, [(i, (i + k) % n) for i in range(n)])


def swap(x, axis, bit):
    n = lax.axis_size(axis)
    return lax.ppermute(x, axis, [(i, i ^ bit) for i in range(n)])


def pick(x, i):
    return lax.dynamic_index_in_dim(x, i, 0, False)


def body(
    residual, head_partials, norm_gain, routes, route_weights, w_gate, w_up, w_down, expert_scale
):
    n_e, n_c = lax.axis_size("expert"), lax.axis_size("cuts")
    e, c = lax.axis_index("expert"), lax.axis_index("cuts")
    own_rows, width = residual.shape
    rows_e = own_rows * n_c
    part = width // n_c
    block = w_gate.shape[1]
    rows = rows_e * n_e
    b, h = c & 1, c >> 1

    share = jnp.sum(
        jnp.where(
            routes[:, :, None] == jnp.arange(EXPERTS, dtype=jnp.int32), route_weights[:, :, None], 0.0
        ),
        1,
    )
    share = lax.all_gather(share, ("expert", "cuts"), axis=0, tiled=True)

    y = head_partials.reshape(rows_e, width)
    mine = lax.dynamic_slice_in_dim(y, c * own_rows, own_rows, 0) + residual.astype(f32)
    y = lax.dynamic_update_slice_in_dim(y, mine, c * own_rows, 0)
    y = y.reshape(rows_e, n_c // 2, 2, part).transpose(2, 1, 0, 3)
    y = pick(y, b) + swap(pick(y, 1 - b), "cuts", 1)
    y = pick(y, h) + swap(pick(y, 1 - h), "cuts", 2)
    own_stream = y.astype(bf16)

    if n_e <= 8:
        pieces = [own_stream] + [shift(own_stream, "expert", k) for k in range(1, n_e)]
        stacked = jnp.stack(pieces)
        order = (e - jnp.arange(n_e)) % n_e
        stream = jnp.take(stacked, order, axis=0).reshape(rows, part)
    else:
        stream = lax.all_gather(own_stream, "expert", axis=0, tiled=True)
    sf = stream.astype(f32)
    square = jnp.sum(sf * sf, 1, keepdims=True)
    square = square + swap(square, "cuts", 1)
    square = square + swap(square, "cuts", 2)
    factor = lax.rsqrt(square / width + 1e-06)
    gain = lax.dynamic_slice_in_dim(norm_gain, c * part, part, 0)
    x = (sf * gain).astype(bf16)

    def product(w):
        p = jnp.dot(x, w, preferred_element_type=f32).astype(bf16)
        p = p.reshape(rows, n_c // 2, 2, block // n_c).transpose(2, 1, 0, 3)
        return p

    g, u = product(w_gate), product(w_up)
    p = jnp.stack([g, u], 2)
    p = pick(p, b).astype(f32) + swap(pick(p, 1 - b), "cuts", 1).astype(f32)
    keep, send = pick(p, h), pick(p, 1 - h).astype(bf16)
    p = keep + swap(send, "cuts", 2).astype(f32)
    g, u = p[0] * factor, p[1] * factor
    unit = e * block + (h * 2 + b) * (block // n_c) + jnp.arange(block // n_c, dtype=jnp.int32)
    coefficient = share * expert_scale
    coefficient = jnp.dot(
        coefficient,
        (jnp.arange(EXPERTS, dtype=jnp.int32)[:, None] == (unit // FH)[None, :]).astype(f32),
        precision=lax.Precision.HIGHEST,
    )
    hidden = (jax.nn.silu(g) * u * coefficient).astype(bf16)
    other = swap(hidden, "cuts", 2)
    pair = jnp.where(h == 0, jnp.stack([hidden, other]), jnp.stack([other, hidden]))
    other = swap(pair, "cuts", 1)
    quad = jnp.where(b == 0, jnp.stack([pair, other], 1), jnp.stack([other, pair], 1))
    hidden = quad.transpose(2, 0, 1, 3).reshape(rows, block)
    out = jnp.dot(hidden, w_down, preferred_element_type=f32)

    if n_e <= 8:
        out = out.reshape(n_e, rows_e, part)
        total = pick(out, e)
        for k in range(1, n_e):
            total = total + shift(pick(out, (e + k) % n_e).astype(bf16), "expert", k).astype(f32)
    else:
        total = lax.psum_scatter(out, "expert", scatter_dimension=0, tiled=True)
    mixed = (own_stream.astype(f32) + total).astype(bf16)
    mixed = lax.all_to_all(
        mixed.reshape(n_c, own_rows, part), "cuts", split_axis=0, concat_axis=0, tiled=True
    )
    return mixed.transpose(1, 0, 2).reshape(own_rows, width)


MIB = 1 << 20
VM = pl.BlockSpec(memory_space=pltpu.VMEM)
PAD = 128
COVER = 1 << 33


HB = pl.BlockSpec(memory_space=pltpu.HBM)


def call(kernel, outs, *args, limit=4, scratch=(), far=0, inside=False, cost=1):
    return pl.pallas_call(
        kernel,
        in_specs=[VM] * (len(args) - far) + [HB] * far,
        out_specs=[VM] * len(outs),
        out_shape=[
            o if not isinstance(o, tuple) else pltpu.VMEM(*o) if inside else jax.ShapeDtypeStruct(*o)
            for o in outs
        ],
        scratch_shapes=list(scratch),
        cost_estimate=pl.CostEstimate(flops=cost, bytes_accessed=1, transcendentals=0),
        compiler_params=pltpu.CompilerParams(vmem_limit_bytes=limit * MIB),
    )(*args)


def halves(v):
    high = v.astype(bf16)
    return high, (v - high.astype(f32)).astype(bf16)


def column(table, i):
    lane = lax.broadcasted_iota(jnp.int32, table.shape, 1)
    return jnp.sum(jnp.where(lane == i, table, 0.0), 1, keepdims=True)


def split_kernel(*refs):
    inputs, outs, scratch, sem = refs[:6], refs[6:10], refs[10:16], refs[16]
    heads, residual, routes, weights, gains, scales = scratch
    send, keep, gain, scale = outs
    copies = [
        pltpu.make_async_copy(a.at[0] if i == 0 else a, t, sem.at[i])
        for i, (a, t) in enumerate(zip(inputs, scratch))
    ]
    for copy in copies:
        copy.start()
    for copy in copies:
        copy.wait()
    c = lax.axis_index("cuts")
    b = c & 1
    rows, width = heads.shape
    own = residual.shape[0]
    n_c = rows // own
    part = width // n_c
    at = lax.broadcasted_iota(jnp.int32, (rows, 1), 0) // own == c

    def wide(v):
        return jnp.where(at, jnp.concatenate([v] * n_c, 0), 0.0)

    for x in range(n_c // 2):
        low = pl.ds(2 * x * part, part)
        high = pl.ds((2 * x + 1) * part, part)
        v0 = heads[:, low] + wide(residual[:, low].astype(f32))
        v1 = heads[:, high] + wide(residual[:, high].astype(f32))
        to = pl.ds(x * part, part)
        keep[:, to] = jnp.where(b == 0, v0, v1)
        send[:, to] = jnp.where(b == 0, v1, v0)
    lane = lax.broadcasted_iota(jnp.int32, (own, PAD), 1)
    share = jnp.zeros((own, PAD), f32)
    for k in range(routes.shape[1]):
        share = share + jnp.where(lane == routes[:, k : k + 1], weights[:, k : k + 1], 0.0)
    share = wide(share)
    end = pl.ds(n_c // 2 * part, PAD)
    keep[:, end] = share
    send[:, end] = share
    scale[...] = scales[...]
    lines = part // PAD
    for i in range(lines):
        gain[:, i * PAD : (i + 1) * PAD] = gains[pl.ds(c * lines + i, 1), :]


def share_parts(v):
    high, low = halves(v)
    lane = lax.broadcasted_iota(jnp.int32, v.shape, 1)
    low = pltpu.roll(jnp.where(lane < EXPERTS, low.astype(f32), 0.0), EXPERTS, 1)
    return (jnp.where(lane < EXPERTS, high.astype(f32), 0.0) + low).astype(bf16)


def share_sum(t):
    t = t.astype(f32)
    lane = lax.broadcasted_iota(jnp.int32, t.shape, 1)
    return jnp.where(lane < EXPERTS, t + pltpu.roll(t, PAD - EXPERTS, 1), 0.0)


def join_kernel(keep, got, send, left):
    h = lax.axis_index("cuts") >> 1
    part = left.shape[1] - PAD
    v0 = keep[:, :part] + got[:, :part]
    v1 = keep[:, part : 2 * part] + got[:, part : 2 * part]
    share = keep[:, 2 * part :] + got[:, 2 * part :]
    left[:, :part] = jnp.where(h == 0, v0, v1)
    send[:, :part] = jnp.where(h == 0, v1, v0).astype(bf16)
    left[:, part:] = share
    send[:, part:] = share_parts(share)


def stream_kernel(left, got, out):
    part = left.shape[1] - PAD
    out[:, :part] = (left[:, :part] + got[:, :part].astype(f32)).astype(bf16)
    out[:, part:] = share_parts(left[:, part:] + share_sum(got[:, part:]))


def expert_of(pair, other):
    b = lax.axis_index("cuts") & 1
    return 2 * pair + (1 - b if other else b)


PIECES = ((0, True), (0, False), (1, True), (1, False))


def load_kernel(w_up, after, w_gate, *refs):
    gates, ups, sem = refs[:3], refs[3:7], refs[7]
    copies = []
    for w, outs, split in ((w_gate, gates, SPLIT), (w_up, ups, 1)):
        for out, piece in zip(outs, PIECES):
            at = pl.ds(pl.multiple_of(expert_of(*piece) * FH, FH), FH)
            step = w.shape[0] // split
            for p in range(split):
                rows = pl.ds(p * step, step)
                n = len(copies)
                copies.append(pltpu.make_async_copy(w.at[rows, at], out.at[rows], sem.at[n]))
    for copy in copies:
        copy.start()
    for copy in copies:
        copy.wait()


def load_down_kernel(after, w_down, *refs):
    outs, token, sem = refs[:-2], refs[-2], refs[-1]
    copies = []
    for i, (pair, other) in enumerate(((0, False), (0, True), (1, False), (1, True))):
        at = pl.ds(pl.multiple_of(expert_of(pair, other) * FH, FH), FH)
        copies.append(pltpu.make_async_copy(w_down.at[at], outs[i], sem.at[i]))
    for copy in copies:
        copy.start()
    for copy in copies:
        copy.wait()
    token[...] = jnp.zeros_like(token)


def expert_product(x, w_gate, w_up, out):
    tile = 256
    for w, base in ((w_gate, 0), (w_up, FH)):
        for i in range(FH // tile):
            p = jnp.dot(x[...], w[:, i * tile : (i + 1) * tile], preferred_element_type=f32)
            out[:, pl.ds(base + i * tile, tile)] = p.astype(out.dtype)


def first_kernel(s0, s1, s2, s3, gain, w_gate, w_up, x, send, share, square):
    part = x.shape[1]
    rows_e = s0.shape[0]
    weight = gain[...]
    for k, s in enumerate((s0, s1, s2, s3)):
        v = s[:, :part].astype(f32)
        at = pl.ds(k * rows_e, rows_e)
        x[at, :] = (v * weight).astype(bf16)
        square[at, :] = jnp.broadcast_to(jnp.sum(v * v, 1, keepdims=True), (rows_e, PAD))
        share[at, :] = share_sum(s[:, part:])
    expert_product(x, w_gate, w_up, send)
    send[:, 2 * FH :] = parts(square[...])


def parts(v):
    high, low = halves(v)
    lane = lax.broadcasted_iota(jnp.int32, v.shape, 1)
    return jnp.where(lane == 0, high.astype(f32), low.astype(f32)).astype(bf16)


def pair_sum(t):
    lane = lax.broadcasted_iota(jnp.int32, t.shape, 1)
    return jnp.broadcast_to(jnp.sum(jnp.where(lane < 2, t, 0.0), 1, keepdims=True), t.shape)


def product_kernel(x, w_gate, w_up, out):
    expert_product(x, w_gate, w_up, out)


def product_stream_kernel(x, up, gate_hbm, out, gate, sem):
    at = pl.ds(pl.multiple_of(expert_of(1, False) * FH, FH), FH)
    step = 256
    copies = []
    for p in range(x.shape[1] // step):
        rows = pl.ds(p * step, step)
        copies.append(pltpu.make_async_copy(gate_hbm.at[rows, at], gate.at[rows], sem.at[p]))
    for copy in copies:
        copy.start()
    for i in range(FH // step):
        to = pl.ds(i * step, step)
        out[:, pl.ds(FH + i * step, step)] = jnp.dot(x[...], up[:, to], preferred_element_type=f32)
    for p, copy in enumerate(copies):
        rows = pl.ds(p * step, step)
        copy.wait()
        v = jnp.dot(x[:, rows], gate[rows, :], preferred_element_type=f32)
        out[:, :FH] = v if p == 0 else out[:, :FH] + v


def own_expert(pair):
    e = lax.axis_index("expert")
    return e * (EXPERTS // lax.axis_size("expert")) + expert_of(pair, False)


def places(share, own_rows, slots):
    rows = share.shape[0]
    on = jnp.where(share != 0.0, 1.0, 0.0)
    row = lax.broadcasted_iota(jnp.int32, (rows, 1), 0)
    within = row % own_rows
    before = jnp.zeros_like(on)
    wide = jnp.broadcast_to(on, (rows, PAD))
    for d in range(1, own_rows):
        before = before + jnp.where(within >= d, pltpu.roll(wide, d, 0)[:, :1], 0.0)
    slot = row // own_rows * MOST + before.astype(jnp.int32)
    at = lax.broadcasted_iota(jnp.int32, (rows, slots), 1)
    return jnp.where((at == slot) & (on != 0.0), 1.0, 0.0).astype(bf16)


def packed(v, where):
    dims = (((0,), (0,)), ((), ()))
    return lax.dot_general(where, v, dims, preferred_element_type=f32).astype(bf16)


def payload(v, square, share, pair, own_rows, send, place):
    where = places(column(share[...], own_expert(pair)), own_rows, send.shape[0])
    place[...] = where
    send[:, : 2 * FH] = packed(v.astype(bf16), where)
    send[:, 2 * FH :] = packed(parts(square), where)


def first_sum_kernel(own_rows, keep, got, square, share, total, send, square_out, place):
    v = keep[...] + got[:, : 2 * FH].astype(f32)
    total[...] = v
    s = square[...] + pair_sum(got[:, 2 * FH :].astype(f32))
    square_out[...] = s
    payload(v, s, share, 0, own_rows, send, place)


def sum_kernel(own_rows, keep, got, square, share, total, send, place):
    v = keep[...] + got[...].astype(f32)
    total[...] = v
    payload(v, square[...], share, 1, own_rows, send, place)


def hidden_kernel(pair, width, total, got, square, place, share, scale, after, out):
    squares = pair_sum(jnp.dot(place[...], got[:, 2 * FH :], preferred_element_type=f32))
    factor = lax.rsqrt((square[...] + squares) / width + 1e-06)[:, :1]
    expert = own_expert(pair)
    coefficient = column(share[...], expert) * column(scale[...], expert)
    v = jnp.dot(place[...], got[:, : 2 * FH], preferred_element_type=f32)
    v = (total[...] + v) * factor
    g, u = v[:, :FH], v[:, FH:]
    out[...] = (g / (1.0 + jnp.exp(-g)) * u * coefficient).astype(bf16)


def down_kernel(last, *refs):
    if last:
        hidden, w_down, before, o0, o1, o2, o3 = refs
    elif len(refs) == 4:
        hidden, w_down, before, out = refs
    else:
        (hidden, w_down, out), before = refs, None
    tile = 256
    for i in range(w_down.shape[1] // tile):
        cols = pl.ds(i * tile, tile)
        p = jnp.dot(hidden[...], w_down[:, cols], preferred_element_type=f32)
        if before is not None:
            p = p + before[:, cols]
        if last:
            r = o0.shape[0]
            for k, o in enumerate((o0, o1, o2, o3)):
                o[:, cols] = p[k * r : (k + 1) * r].astype(o.dtype)
        else:
            out[:, cols] = p


def mixed_kernel(stream, own, r3, r2, r1, m0, m1, m2, m3):
    c = lax.axis_index("cuts")
    part = own.shape[1]
    v = stream[:, :part].astype(f32) + own[...]
    for r in (r1, r2, r3):
        v = v + r[...].astype(f32)
    n = m0.shape[0]
    blocks = [v[k * n : (k + 1) * n] for k in range(4)]
    for k, m in enumerate((m0, m1, m2, m3)):
        to = c ^ k
        t = jnp.where(to < 2, jnp.where(to == 0, blocks[0], blocks[1]),
                      jnp.where(to == 2, blocks[2], blocks[3]))
        m[...] = t.astype(bf16)


def final_kernel(m0, m1, m2, m3, out):
    c = lax.axis_index("cuts")
    part = m0.shape[1]
    p = [m[...].astype(f32) for m in (m0, m1, m2, m3)]
    for s in range(4):
        k = c ^ s
        t = jnp.where(k < 2, jnp.where(k == 0, p[0], p[1]), jnp.where(k == 2, p[2], p[3]))
        out[:, s * part : (s + 1) * part] = t.astype(bf16)


def fast_body(
    residual, head_partials, norm_gain, routes, route_weights, w_gate, w_up, w_down, expert_scale
):
    own_rows, width = residual.shape
    rows_e = 4 * own_rows
    part = width // 4
    rows = 4 * rows_e
    slots = rows // own_rows * MOST
    weight = pltpu.VMEM((part, FH), bf16)

    cut = (rows_e, 2 * part + PAD)
    gains, scales = norm_gain.reshape(width // PAD, PAD), expert_scale.reshape(1, EXPERTS)
    send, keep, gain, scale = call(
        split_kernel, [(cut, f32)] * 2 + [((1, part), f32), ((1, EXPERTS), f32)],
        head_partials, residual, routes, route_weights, gains, scales,
        far=6, limit=62, inside=True,
        scratch=[
            pltpu.VMEM((rows_e, width), f32), pltpu.VMEM(residual.shape, bf16),
            pltpu.VMEM(routes.shape, jnp.int32), pltpu.VMEM(route_weights.shape, f32),
            pltpu.VMEM(gains.shape, f32), pltpu.VMEM(scales.shape, f32),
            pltpu.SemaphoreType.DMA((6,)),
        ],
    )
    cut = (rows_e, part + PAD)
    send, left = call(join_kernel, [(cut, bf16), (cut, f32)], keep, swap(send, "cuts", 1), cost=COVER)
    got = swap(send, "cuts", 2)
    (s0,) = call(stream_kernel, [(cut, bf16)], left, got, cost=COVER // 4)
    s3, s2, s1 = [swap(s0, "expert", k) for k in (3, 2, 1)]
    ga0, gb0, ga1, ua0, ub0, ua1, ub1 = call(
        load_kernel, [weight] * 7, w_up, s0, w_gate, far=2, limit=4,
        scratch=[pltpu.SemaphoreType.DMA((3 * SPLIT + 4,))],
    )
    x, send, share, square = call(
        first_kernel,
        [((rows, part), bf16), ((rows, 2 * FH + PAD), bf16), ((rows, PAD), f32), ((rows, PAD), f32)],
        s0, s1, s2, s3, gain, ga0, ua0,
    )
    got = swap(send, "cuts", 1)
    full = ((rows, 2 * FH), f32)
    (keep,) = call(product_kernel, [full], x, gb0, ub0)
    table = ((rows, PAD), f32)
    sent_all = ((rows, 2 * FH), bf16)
    place = ((rows, slots), bf16)
    sent = ((slots, 2 * FH + PAD), bf16)
    total0, send, square, place0 = call(
        functools.partial(first_sum_kernel, own_rows),
        [full, sent, table, place], keep, got, square, share,
    )
    got0 = swap(send, "cuts", 2)
    (send,) = call(product_kernel, [sent_all], x, ga1, ua1)
    got = swap(send, "cuts", 1)
    (keep,) = call(
        product_stream_kernel, [full], x, ub1, w_gate, far=1, limit=47,
        scratch=[pltpu.VMEM((part, FH), bf16), pltpu.SemaphoreType.DMA((part // 256,))],
    )
    total1, send, place1 = call(
        functools.partial(sum_kernel, own_rows), [full, sent, place], keep, got, square, share
    )
    got1 = swap(send, "cuts", 2)
    d0, d1, d2, d3, after = pl.pallas_call(
        load_down_kernel,
        in_specs=[HB] * 2,
        out_specs=[VM] * 5,
        out_shape=[pltpu.VMEM((FH, part), bf16)] * 4 + [jax.ShapeDtypeStruct((8, PAD), f32)],
        scratch_shapes=[pltpu.SemaphoreType.DMA((4,))],
        cost_estimate=pl.CostEstimate(flops=1, bytes_accessed=1, transcendentals=0),
        compiler_params=pltpu.CompilerParams(vmem_limit_bytes=34 * MIB),
    )(send, w_down)

    half = ((rows, FH), bf16)
    out = ((rows, part), f32)
    (h0,) = call(
        functools.partial(hidden_kernel, 0, width), [half],
        total0, got0, square, place0, share, scale, after,
    )
    g0 = swap(h0, "cuts", 1)
    (t,) = call(functools.partial(down_kernel, False), [out], h0, d0)
    (t,) = call(functools.partial(down_kernel, False), [out], g0, d1, t)
    (h1,) = call(
        functools.partial(hidden_kernel, 1, width), [half],
        total1, got1, square, place1, share, scale, after,
    )
    g1 = swap(h1, "cuts", 1)
    (t,) = call(functools.partial(down_kernel, False), [out], h1, d2, t)
    o0, o1, o2, o3 = call(
        functools.partial(down_kernel, True),
        [((rows_e, part), f32)] + [((rows_e, part), bf16)] * 3,
        g1, d3, t,
    )
    r3, r2, r1 = [swap(o, "expert", k) for k, o in ((3, o3), (2, o2), (1, o1))]
    m0, m1, m2, m3 = call(mixed_kernel, [((own_rows, part), bf16)] * 4, s0, o0, r3, r2, r1)
    m2, m3, m1 = [swap(m, "cuts", k) for k, m in ((2, m2), (3, m3), (1, m1))]
    (mixed,) = call(final_kernel, [((own_rows, width), bf16)], m0, m1, m2, m3)
    return mixed


def solution(mesh):
    in_specs = (
        P(("group", "expert", "cuts"), None),
        P("cuts", ("group", "expert"), None),
        P(),
        P(("group", "expert", "cuts"), None),
        P(("group", "expert", "cuts"), None),
        P("cuts", "expert"),
        P("cuts", "expert"),
        P("expert", "cuts"),
        P(),
    )
    out_specs = P(("group", "expert", "cuts"), None)
    small = mesh.shape["expert"] == 4 and mesh.shape["cuts"] == 4
    return jax.shard_map(
        fast_body if small else body, mesh=mesh, in_specs=in_specs, out_specs=out_specs, check_vma=False
    )
```

```python
import functools

import jax
import jax.numpy as jnp
from jax import lax
from jax.experimental import pallas as pl
from jax.experimental.pallas import tpu as pltpu
from jax.sharding import PartitionSpec as P

FH = 1024
EXPERTS = 16
SPLIT = 4
MOST = 3
bf16, f32 = jnp.bfloat16, jnp.float32


def shift(x, axis, k):
    n = lax.axis_size(axis)
    return lax.ppermute(x, axis, [(i, (i + k) % n) for i in range(n)])


def swap(x, axis, bit):
    n = lax.axis_size(axis)
    return lax.ppermute(x, axis, [(i, i ^ bit) for i in range(n)])


def pick(x, i):
    return lax.dynamic_index_in_dim(x, i, 0, False)


def body(
    residual, head_partials, norm_gain, routes, route_weights, w_gate, w_up, w_down, expert_scale
):
    n_e, n_c = lax.axis_size("expert"), lax.axis_size("cuts")
    e, c = lax.axis_index("expert"), lax.axis_index("cuts")
    own_rows, width = residual.shape
    rows_e = own_rows * n_c
    part = width // n_c
    block = w_gate.shape[1]
    rows = rows_e * n_e
    b, h = c & 1, c >> 1

    share = jnp.sum(
        jnp.where(
            routes[:, :, None] == jnp.arange(EXPERTS, dtype=jnp.int32), route_weights[:, :, None], 0.0
        ),
        1,
    )
    share = lax.all_gather(share, ("expert", "cuts"), axis=0, tiled=True)

    y = head_partials.reshape(rows_e, width)
    mine = lax.dynamic_slice_in_dim(y, c * own_rows, own_rows, 0) + residual.astype(f32)
    y = lax.dynamic_update_slice_in_dim(y, mine, c * own_rows, 0)
    y = y.reshape(rows_e, n_c // 2, 2, part).transpose(2, 1, 0, 3)
    y = pick(y, b) + swap(pick(y, 1 - b), "cuts", 1)
    y = pick(y, h) + swap(pick(y, 1 - h), "cuts", 2)
    own_stream = y.astype(bf16)

    if n_e <= 8:
        pieces = [own_stream] + [shift(own_stream, "expert", k) for k in range(1, n_e)]
        stacked = jnp.stack(pieces)
        order = (e - jnp.arange(n_e)) % n_e
        stream = jnp.take(stacked, order, axis=0).reshape(rows, part)
    else:
        stream = lax.all_gather(own_stream, "expert", axis=0, tiled=True)
    sf = stream.astype(f32)
    square = jnp.sum(sf * sf, 1, keepdims=True)
    square = square + swap(square, "cuts", 1)
    square = square + swap(square, "cuts", 2)
    factor = lax.rsqrt(square / width + 1e-06)
    gain = lax.dynamic_slice_in_dim(norm_gain, c * part, part, 0)
    x = (sf * gain).astype(bf16)

    def product(w):
        p = jnp.dot(x, w, preferred_element_type=f32).astype(bf16)
        p = p.reshape(rows, n_c // 2, 2, block // n_c).transpose(2, 1, 0, 3)
        return p

    g, u = product(w_gate), product(w_up)
    p = jnp.stack([g, u], 2)
    p = pick(p, b).astype(f32) + swap(pick(p, 1 - b), "cuts", 1).astype(f32)
    keep, send = pick(p, h), pick(p, 1 - h).astype(bf16)
    p = keep + swap(send, "cuts", 2).astype(f32)
    g, u = p[0] * factor, p[1] * factor
    unit = e * block + (h * 2 + b) * (block // n_c) + jnp.arange(block // n_c, dtype=jnp.int32)
    coefficient = share * expert_scale
    coefficient = jnp.dot(
        coefficient,
        (jnp.arange(EXPERTS, dtype=jnp.int32)[:, None] == (unit // FH)[None, :]).astype(f32),
        precision=lax.Precision.HIGHEST,
    )
    hidden = (jax.nn.silu(g) * u * coefficient).astype(bf16)
    other = swap(hidden, "cuts", 2)
    pair = jnp.where(h == 0, jnp.stack([hidden, other]), jnp.stack([other, hidden]))
    other = swap(pair, "cuts", 1)
    quad = jnp.where(b == 0, jnp.stack([pair, other], 1), jnp.stack([other, pair], 1))
    hidden = quad.transpose(2, 0, 1, 3).reshape(rows, block)
    out = jnp.dot(hidden, w_down, preferred_element_type=f32)

    if n_e <= 8:
        out = out.reshape(n_e, rows_e, part)
        total = pick(out, e)
        for k in range(1, n_e):
            total = total + shift(pick(out, (e + k) % n_e).astype(bf16), "expert", k).astype(f32)
    else:
        total = lax.psum_scatter(out, "expert", scatter_dimension=0, tiled=True)
    mixed = (own_stream.astype(f32) + total).astype(bf16)
    mixed = lax.all_to_all(
        mixed.reshape(n_c, own_rows, part), "cuts", split_axis=0, concat_axis=0, tiled=True
    )
    return mixed.transpose(1, 0, 2).reshape(own_rows, width)


MIB = 1 << 20
VM = pl.BlockSpec(memory_space=pltpu.VMEM)
PAD = 128
COVER = 1 << 33


HB = pl.BlockSpec(memory_space=pltpu.HBM)


def call(kernel, outs, *args, limit=4, scratch=(), far=0, inside=False, cost=1):
    return pl.pallas_call(
        kernel,
        in_specs=[VM] * (len(args) - far) + [HB] * far,
        out_specs=[VM] * len(outs),
        out_shape=[
            o if not isinstance(o, tuple) else pltpu.VMEM(*o) if inside else jax.ShapeDtypeStruct(*o)
            for o in outs
        ],
        scratch_shapes=list(scratch),
        cost_estimate=pl.CostEstimate(flops=cost, bytes_accessed=1, transcendentals=0),
        compiler_params=pltpu.CompilerParams(vmem_limit_bytes=limit * MIB),
    )(*args)


def halves(v):
    high = v.astype(bf16)
    return high, (v - high.astype(f32)).astype(bf16)


def column(table, i):
    lane = lax.broadcasted_iota(jnp.int32, table.shape, 1)
    return jnp.sum(jnp.where(lane == i, table, 0.0), 1, keepdims=True)


def split_kernel(*refs):
    inputs, outs, scratch, sem = refs[:6], refs[6:10], refs[10:16], refs[16]
    heads, residual, routes, weights, gains, scales = scratch
    send, keep, gain, scale = outs
    copies = [
        pltpu.make_async_copy(a.at[0] if i == 0 else a, t, sem.at[i])
        for i, (a, t) in enumerate(zip(inputs, scratch))
    ]
    for copy in copies:
        copy.start()
    for copy in copies:
        copy.wait()
    c = lax.axis_index("cuts")
    b = c & 1
    rows, width = heads.shape
    own = residual.shape[0]
    n_c = rows // own
    part = width // n_c
    at = lax.broadcasted_iota(jnp.int32, (rows, 1), 0) // own == c

    def wide(v):
        return jnp.where(at, jnp.concatenate([v] * n_c, 0), 0.0)

    for x in range(n_c // 2):
        low = pl.ds(2 * x * part, part)
        high = pl.ds((2 * x + 1) * part, part)
        v0 = heads[:, low] + wide(residual[:, low].astype(f32))
        v1 = heads[:, high] + wide(residual[:, high].astype(f32))
        to = pl.ds(x * part, part)
        keep[:, to] = jnp.where(b == 0, v0, v1)
        send[:, to] = jnp.where(b == 0, v1, v0)
    lane = lax.broadcasted_iota(jnp.int32, (own, PAD), 1)
    share = jnp.zeros((own, PAD), f32)
    for k in range(routes.shape[1]):
        share = share + jnp.where(lane == routes[:, k : k + 1], weights[:, k : k + 1], 0.0)
    share = wide(share)
    end = pl.ds(n_c // 2 * part, PAD)
    keep[:, end] = share
    send[:, end] = share
    scale[...] = scales[...]
    lines = part // PAD
    for i in range(lines):
        gain[:, i * PAD : (i + 1) * PAD] = gains[pl.ds(c * lines + i, 1), :]


def share_parts(v):
    high, low = halves(v)
    lane = lax.broadcasted_iota(jnp.int32, v.shape, 1)
    low = pltpu.roll(jnp.where(lane < EXPERTS, low.astype(f32), 0.0), EXPERTS, 1)
    return (jnp.where(lane < EXPERTS, high.astype(f32), 0.0) + low).astype(bf16)


def share_sum(t):
    t = t.astype(f32)
    lane = lax.broadcasted_iota(jnp.int32, t.shape, 1)
    return jnp.where(lane < EXPERTS, t + pltpu.roll(t, PAD - EXPERTS, 1), 0.0)


def join_kernel(keep, got, send, left):
    h = lax.axis_index("cuts") >> 1
    part = left.shape[1] - PAD
    v0 = keep[:, :part] + got[:, :part]
    v1 = keep[:, part : 2 * part] + got[:, part : 2 * part]
    share = keep[:, 2 * part :] + got[:, 2 * part :]
    left[:, :part] = jnp.where(h == 0, v0, v1)
    send[:, :part] = jnp.where(h == 0, v1, v0).astype(bf16)
    left[:, part:] = share
    send[:, part:] = share_parts(share)


def stream_kernel(left, got, out):
    part = left.shape[1] - PAD
    out[:, :part] = (left[:, :part] + got[:, :part].astype(f32)).astype(bf16)
    out[:, part:] = share_parts(left[:, part:] + share_sum(got[:, part:]))


def expert_of(pair, other):
    b = lax.axis_index("cuts") & 1
    return 2 * pair + (1 - b if other else b)


PIECES = ((0, True), (0, False), (1, True), (1, False))


def load_kernel(w_up, after, w_gate, *refs):
    gates, ups, sem = refs[:3], refs[3:7], refs[7]
    copies = []
    for w, outs, split in ((w_gate, gates, SPLIT), (w_up, ups, 1)):
        for out, piece in zip(outs, PIECES):
            at = pl.ds(pl.multiple_of(expert_of(*piece) * FH, FH), FH)
            step = w.shape[0] // split
            for p in range(split):
                rows = pl.ds(p * step, step)
                n = len(copies)
                copies.append(pltpu.make_async_copy(w.at[rows, at], out.at[rows], sem.at[n]))
    for copy in copies:
        copy.start()
    for copy in copies:
        copy.wait()


def load_down_kernel(after, w_down, *refs):
    outs, token, sem = refs[:-2], refs[-2], refs[-1]
    copies = []
    for i, (pair, other) in enumerate(((0, False), (0, True), (1, False), (1, True))):
        at = pl.ds(pl.multiple_of(expert_of(pair, other) * FH, FH), FH)
        copies.append(pltpu.make_async_copy(w_down.at[at], outs[i], sem.at[i]))
    for copy in copies:
        copy.start()
    for copy in copies:
        copy.wait()
    token[...] = jnp.zeros_like(token)


def expert_product(x, w_gate, w_up, out):
    tile = 256
    for w, base in ((w_gate, 0), (w_up, FH)):
        for i in range(FH // tile):
            p = jnp.dot(x[...], w[:, i * tile : (i + 1) * tile], preferred_element_type=f32)
            out[:, pl.ds(base + i * tile, tile)] = p.astype(out.dtype)


def first_kernel(s0, s1, s2, s3, gain, w_gate, w_up, x, send, share, square):
    part = x.shape[1]
    rows_e = s0.shape[0]
    weight = gain[...]
    for k, s in enumerate((s0, s1, s2, s3)):
        v = s[:, :part].astype(f32)
        at = pl.ds(k * rows_e, rows_e)
        x[at, :] = (v * weight).astype(bf16)
        square[at, :] = jnp.broadcast_to(jnp.sum(v * v, 1, keepdims=True), (rows_e, PAD))
        share[at, :] = share_sum(s[:, part:])
    expert_product(x, w_gate, w_up, send)
    send[:, 2 * FH :] = parts(square[...])


def parts(v):
    high, low = halves(v)
    lane = lax.broadcasted_iota(jnp.int32, v.shape, 1)
    return jnp.where(lane == 0, high.astype(f32), low.astype(f32)).astype(bf16)


def pair_sum(t):
    lane = lax.broadcasted_iota(jnp.int32, t.shape, 1)
    return jnp.broadcast_to(jnp.sum(jnp.where(lane < 2, t, 0.0), 1, keepdims=True), t.shape)


def product_kernel(x, w_gate, w_up, out):
    expert_product(x, w_gate, w_up, out)


def product_stream_kernel(x, up, gate_hbm, out, gate, sem):
    at = pl.ds(pl.multiple_of(expert_of(1, False) * FH, FH), FH)
    step = 256
    copies = []
    for p in range(x.shape[1] // step):
        rows = pl.ds(p * step, step)
        copies.append(pltpu.make_async_copy(gate_hbm.at[rows, at], gate.at[rows], sem.at[p]))
    for copy in copies:
        copy.start()
    for i in range(FH // step):
        to = pl.ds(i * step, step)
        out[:, pl.ds(FH + i * step, step)] = jnp.dot(x[...], up[:, to], preferred_element_type=f32)
    for p, copy in enumerate(copies):
        rows = pl.ds(p * step, step)
        copy.wait()
        v = jnp.dot(x[:, rows], gate[rows, :], preferred_element_type=f32)
        out[:, :FH] = v if p == 0 else out[:, :FH] + v


def own_expert(pair):
    e = lax.axis_index("expert")
    return e * (EXPERTS // lax.axis_size("expert")) + expert_of(pair, False)


def places(share, own_rows, slots):
    rows = share.shape[0]
    on = jnp.where(share != 0.0, 1.0, 0.0)
    row = lax.broadcasted_iota(jnp.int32, (rows, 1), 0)
    within = row % own_rows
    before = jnp.zeros_like(on)
    wide = jnp.broadcast_to(on, (rows, PAD))
    for d in range(1, own_rows):
        before = before + jnp.where(within >= d, pltpu.roll(wide, d, 0)[:, :1], 0.0)
    slot = row // own_rows * MOST + before.astype(jnp.int32)
    at = lax.broadcasted_iota(jnp.int32, (rows, slots), 1)
    return jnp.where((at == slot) & (on != 0.0), 1.0, 0.0).astype(bf16)


def packed(v, where):
    dims = (((0,), (0,)), ((), ()))
    return lax.dot_general(where, v, dims, preferred_element_type=f32).astype(bf16)


def payload(v, share, pair, own_rows, send, place):
    where = places(column(share[...], own_expert(pair)), own_rows, send.shape[0])
    place[...] = where
    send[:, : 2 * FH] = packed(v.astype(bf16), where)


def lanes(shape):
    lane = lax.broadcasted_iota(jnp.int32, shape, 1)
    row = lax.broadcasted_iota(jnp.int32, shape, 0)
    return lane == row, lane == row + shape[0]


def first_sum_kernel(own_rows, keep, got, square, share, total, send, square_out, place):
    v = keep[...] + got[:, : 2 * FH].astype(f32)
    total[...] = v
    payload(v, share, 0, own_rows, send, place)
    s = square[...] + pair_sum(got[:, 2 * FH :].astype(f32))
    square_out[...] = s
    high, low = halves(s)
    at_high, at_low = lanes(s.shape)
    t = jnp.where(at_high, high.astype(f32), jnp.where(at_low, low.astype(f32), 0.0))
    t = jnp.broadcast_to(jnp.sum(t, 0, keepdims=True), (send.shape[0], PAD))
    send[:, 2 * FH :] = t.astype(bf16)


def sum_kernel(own_rows, keep, got, share, total, send, place):
    v = keep[...] + got[...].astype(f32)
    total[...] = v
    payload(v, share, 1, own_rows, send, place)


def hidden_kernel(pair, width, total, got, first, square, place, share, scale, after, out):
    at_high, at_low = lanes(square.shape)
    t = jnp.broadcast_to(first[:16, 2 * FH :].astype(f32)[:1], square.shape)
    squares = square[:, :1] + jnp.sum(jnp.where(at_high | at_low, t, 0.0), 1, keepdims=True)
    factor = lax.rsqrt(squares / width + 1e-06)
    expert = own_expert(pair)
    coefficient = column(share[...], expert) * column(scale[...], expert)
    v = jnp.dot(place[...], got[:, : 2 * FH], preferred_element_type=f32)
    v = (total[...] + v) * factor
    g, u = v[:, :FH], v[:, FH:]
    out[...] = (g / (1.0 + jnp.exp(-g)) * u * coefficient).astype(bf16)


def down_kernel(last, *refs):
    if last:
        hidden, w_down, before, o0, o1, o2, o3 = refs
    elif len(refs) == 4:
        hidden, w_down, before, out = refs
    else:
        (hidden, w_down, out), before = refs, None
    tile = 256
    for i in range(w_down.shape[1] // tile):
        cols = pl.ds(i * tile, tile)
        p = jnp.dot(hidden[...], w_down[:, cols], preferred_element_type=f32)
        if before is not None:
            p = p + before[:, cols]
        if last:
            r = o0.shape[0]
            for k, o in enumerate((o0, o1, o2, o3)):
                o[:, cols] = p[k * r : (k + 1) * r].astype(o.dtype)
        else:
            out[:, cols] = p


def mixed_kernel(stream, own, r3, r2, r1, m0, m1, m2, m3):
    c = lax.axis_index("cuts")
    part = own.shape[1]
    v = stream[:, :part].astype(f32) + own[...]
    for r in (r1, r2, r3):
        v = v + r[...].astype(f32)
    n = m0.shape[0]
    blocks = [v[k * n : (k + 1) * n] for k in range(4)]
    for k, m in enumerate((m0, m1, m2, m3)):
        to = c ^ k
        t = jnp.where(to < 2, jnp.where(to == 0, blocks[0], blocks[1]),
                      jnp.where(to == 2, blocks[2], blocks[3]))
        m[...] = t.astype(bf16)


def final_kernel(m0, m1, m2, m3, out):
    c = lax.axis_index("cuts")
    part = m0.shape[1]
    p = [m[...].astype(f32) for m in (m0, m1, m2, m3)]
    for s in range(4):
        k = c ^ s
        t = jnp.where(k < 2, jnp.where(k == 0, p[0], p[1]), jnp.where(k == 2, p[2], p[3]))
        out[:, s * part : (s + 1) * part] = t.astype(bf16)


def fast_body(
    residual, head_partials, norm_gain, routes, route_weights, w_gate, w_up, w_down, expert_scale
):
    own_rows, width = residual.shape
    rows_e = 4 * own_rows
    part = width // 4
    rows = 4 * rows_e
    slots = rows // own_rows * MOST
    weight = pltpu.VMEM((part, FH), bf16)

    cut = (rows_e, 2 * part + PAD)
    gains, scales = norm_gain.reshape(width // PAD, PAD), expert_scale.reshape(1, EXPERTS)
    send, keep, gain, scale = call(
        split_kernel, [(cut, f32)] * 2 + [((1, part), f32), ((1, EXPERTS), f32)],
        head_partials, residual, routes, route_weights, gains, scales,
        far=6, limit=62, inside=True,
        scratch=[
            pltpu.VMEM((rows_e, width), f32), pltpu.VMEM(residual.shape, bf16),
            pltpu.VMEM(routes.shape, jnp.int32), pltpu.VMEM(route_weights.shape, f32),
            pltpu.VMEM(gains.shape, f32), pltpu.VMEM(scales.shape, f32),
            pltpu.SemaphoreType.DMA((6,)),
        ],
    )
    cut = (rows_e, part + PAD)
    send, left = call(join_kernel, [(cut, bf16), (cut, f32)], keep, swap(send, "cuts", 1), cost=COVER)
    got = swap(send, "cuts", 2)
    (s0,) = call(stream_kernel, [(cut, bf16)], left, got, cost=COVER // 4)
    s3, s2, s1 = [swap(s0, "expert", k) for k in (3, 2, 1)]
    ga0, gb0, ga1, ua0, ub0, ua1, ub1 = call(
        load_kernel, [weight] * 7, w_up, s0, w_gate, far=2, limit=4,
        scratch=[pltpu.SemaphoreType.DMA((3 * SPLIT + 4,))],
    )
    x, send, share, square = call(
        first_kernel,
        [((rows, part), bf16), ((rows, 2 * FH + PAD), bf16), ((rows, PAD), f32), ((rows, PAD), f32)],
        s0, s1, s2, s3, gain, ga0, ua0,
    )
    got = swap(send, "cuts", 1)
    full = ((rows, 2 * FH), f32)
    (keep,) = call(product_kernel, [full], x, gb0, ub0)
    table = ((rows, PAD), f32)
    sent_all = ((rows, 2 * FH), bf16)
    place = ((rows, slots), bf16)
    sent = ((slots, 2 * FH + PAD), bf16)
    total0, send, square, place0 = call(
        functools.partial(first_sum_kernel, own_rows),
        [full, sent, table, place], keep, got, square, share,
    )
    got0 = swap(send, "cuts", 2)
    (send,) = call(product_kernel, [sent_all], x, ga1, ua1)
    got = swap(send, "cuts", 1)
    (keep,) = call(
        product_stream_kernel, [full], x, ub1, w_gate, far=1, limit=47,
        scratch=[pltpu.VMEM((part, FH), bf16), pltpu.SemaphoreType.DMA((part // 256,))],
    )
    total1, send, place1 = call(
        functools.partial(sum_kernel, own_rows), [full, ((slots, 2 * FH), bf16), place], keep, got, share
    )
    got1 = swap(send, "cuts", 2)
    d0, d1, d2, d3, after = pl.pallas_call(
        load_down_kernel,
        in_specs=[HB] * 2,
        out_specs=[VM] * 5,
        out_shape=[pltpu.VMEM((FH, part), bf16)] * 4 + [jax.ShapeDtypeStruct((8, PAD), f32)],
        scratch_shapes=[pltpu.SemaphoreType.DMA((4,))],
        cost_estimate=pl.CostEstimate(flops=1, bytes_accessed=1, transcendentals=0),
        compiler_params=pltpu.CompilerParams(vmem_limit_bytes=34 * MIB),
    )(send, w_down)

    half = ((rows, FH), bf16)
    out = ((rows, part), f32)
    (h0,) = call(
        functools.partial(hidden_kernel, 0, width), [half],
        total0, got0, got0, square, place0, share, scale, after,
    )
    g0 = swap(h0, "cuts", 1)
    (t,) = call(functools.partial(down_kernel, False), [out], h0, d0)
    (h1,) = call(
        functools.partial(hidden_kernel, 1, width), [half],
        total1, got1, got0, square, place1, share, scale, t, far=1,
    )
    (t,) = call(functools.partial(down_kernel, False), [out], g0, d1, t)
    g1 = swap(h1, "cuts", 1)
    (t,) = call(functools.partial(down_kernel, False), [out], h1, d2, t)
    o0, o1, o2, o3 = call(
        functools.partial(down_kernel, True),
        [((rows_e, part), f32)] + [((rows_e, part), bf16)] * 3,
        g1, d3, t,
    )
    r3, r2, r1 = [swap(o, "expert", k) for k, o in ((3, o3), (2, o2), (1, o1))]
    m0, m1, m2, m3 = call(mixed_kernel, [((own_rows, part), bf16)] * 4, s0, o0, r3, r2, r1)
    m2, m3, m1 = [swap(m, "cuts", k) for k, m in ((2, m2), (3, m3), (1, m1))]
    (mixed,) = call(final_kernel, [((own_rows, width), bf16)], m0, m1, m2, m3)
    return mixed


def solution(mesh):
    in_specs = (
        P(("group", "expert", "cuts"), None),
        P("cuts", ("group", "expert"), None),
        P(),
        P(("group", "expert", "cuts"), None),
        P(("group", "expert", "cuts"), None),
        P("cuts", "expert"),
        P("cuts", "expert"),
        P("expert", "cuts"),
        P(),
    )
    out_specs = P(("group", "expert", "cuts"), None)
    small = mesh.shape["expert"] == 4 and mesh.shape["cuts"] == 4

    def pick_body(*args):
        fits = small and 32 * args[0].shape[0] <= PAD
        return (fast_body if fits else body)(*args)

    return jax.shard_map(
        pick_body, mesh=mesh, in_specs=in_specs, out_specs=out_specs, check_vma=False
    )
```

```python
import functools

import jax
import jax.numpy as jnp
from jax import lax
from jax.experimental import pallas as pl
from jax.experimental.pallas import tpu as pltpu
from jax.sharding import PartitionSpec as P

FH = 1024
EXPERTS = 16
SPLIT = 4
MOST = 3
bf16, f32 = jnp.bfloat16, jnp.float32


def shift(x, axis, k):
    n = lax.axis_size(axis)
    return lax.ppermute(x, axis, [(i, (i + k) % n) for i in range(n)])


def swap(x, axis, bit):
    n = lax.axis_size(axis)
    return lax.ppermute(x, axis, [(i, i ^ bit) for i in range(n)])


def pick(x, i):
    return lax.dynamic_index_in_dim(x, i, 0, False)


def body(
    residual, head_partials, norm_gain, routes, route_weights, w_gate, w_up, w_down, expert_scale
):
    n_e, n_c = lax.axis_size("expert"), lax.axis_size("cuts")
    e, c = lax.axis_index("expert"), lax.axis_index("cuts")
    own_rows, width = residual.shape
    rows_e = own_rows * n_c
    part = width // n_c
    block = w_gate.shape[1]
    rows = rows_e * n_e
    b, h = c & 1, c >> 1

    share = jnp.sum(
        jnp.where(
            routes[:, :, None] == jnp.arange(EXPERTS, dtype=jnp.int32), route_weights[:, :, None], 0.0
        ),
        1,
    )
    share = lax.all_gather(share, ("expert", "cuts"), axis=0, tiled=True)

    y = head_partials.reshape(rows_e, width)
    mine = lax.dynamic_slice_in_dim(y, c * own_rows, own_rows, 0) + residual.astype(f32)
    y = lax.dynamic_update_slice_in_dim(y, mine, c * own_rows, 0)
    y = y.reshape(rows_e, n_c // 2, 2, part).transpose(2, 1, 0, 3)
    y = pick(y, b) + swap(pick(y, 1 - b), "cuts", 1)
    y = pick(y, h) + swap(pick(y, 1 - h), "cuts", 2)
    own_stream = y.astype(bf16)

    if n_e <= 8:
        pieces = [own_stream] + [shift(own_stream, "expert", k) for k in range(1, n_e)]
        stacked = jnp.stack(pieces)
        order = (e - jnp.arange(n_e)) % n_e
        stream = jnp.take(stacked, order, axis=0).reshape(rows, part)
    else:
        stream = lax.all_gather(own_stream, "expert", axis=0, tiled=True)
    sf = stream.astype(f32)
    square = jnp.sum(sf * sf, 1, keepdims=True)
    square = square + swap(square, "cuts", 1)
    square = square + swap(square, "cuts", 2)
    factor = lax.rsqrt(square / width + 1e-06)
    gain = lax.dynamic_slice_in_dim(norm_gain, c * part, part, 0)
    x = (sf * gain).astype(bf16)

    def product(w):
        p = jnp.dot(x, w, preferred_element_type=f32).astype(bf16)
        p = p.reshape(rows, n_c // 2, 2, block // n_c).transpose(2, 1, 0, 3)
        return p

    g, u = product(w_gate), product(w_up)
    p = jnp.stack([g, u], 2)
    p = pick(p, b).astype(f32) + swap(pick(p, 1 - b), "cuts", 1).astype(f32)
    keep, send = pick(p, h), pick(p, 1 - h).astype(bf16)
    p = keep + swap(send, "cuts", 2).astype(f32)
    g, u = p[0] * factor, p[1] * factor
    unit = e * block + (h * 2 + b) * (block // n_c) + jnp.arange(block // n_c, dtype=jnp.int32)
    coefficient = share * expert_scale
    coefficient = jnp.dot(
        coefficient,
        (jnp.arange(EXPERTS, dtype=jnp.int32)[:, None] == (unit // FH)[None, :]).astype(f32),
        precision=lax.Precision.HIGHEST,
    )
    hidden = (jax.nn.silu(g) * u * coefficient).astype(bf16)
    other = swap(hidden, "cuts", 2)
    pair = jnp.where(h == 0, jnp.stack([hidden, other]), jnp.stack([other, hidden]))
    other = swap(pair, "cuts", 1)
    quad = jnp.where(b == 0, jnp.stack([pair, other], 1), jnp.stack([other, pair], 1))
    hidden = quad.transpose(2, 0, 1, 3).reshape(rows, block)
    out = jnp.dot(hidden, w_down, preferred_element_type=f32)

    if n_e <= 8:
        out = out.reshape(n_e, rows_e, part)
        total = pick(out, e)
        for k in range(1, n_e):
            total = total + shift(pick(out, (e + k) % n_e).astype(bf16), "expert", k).astype(f32)
    else:
        total = lax.psum_scatter(out, "expert", scatter_dimension=0, tiled=True)
    mixed = (own_stream.astype(f32) + total).astype(bf16)
    mixed = lax.all_to_all(
        mixed.reshape(n_c, own_rows, part), "cuts", split_axis=0, concat_axis=0, tiled=True
    )
    return mixed.transpose(1, 0, 2).reshape(own_rows, width)


MIB = 1 << 20
VM = pl.BlockSpec(memory_space=pltpu.VMEM)
PAD = 128
COVER = 1 << 33


HB = pl.BlockSpec(memory_space=pltpu.HBM)


def call(kernel, outs, *args, limit=4, scratch=(), far=0, inside=False, cost=1):
    return pl.pallas_call(
        kernel,
        in_specs=[VM] * (len(args) - far) + [HB] * far,
        out_specs=[VM] * len(outs),
        out_shape=[
            o if not isinstance(o, tuple) else pltpu.VMEM(*o) if inside else jax.ShapeDtypeStruct(*o)
            for o in outs
        ],
        scratch_shapes=list(scratch),
        cost_estimate=pl.CostEstimate(flops=cost, bytes_accessed=1, transcendentals=0),
        compiler_params=pltpu.CompilerParams(vmem_limit_bytes=limit * MIB),
    )(*args)


def halves(v):
    high = v.astype(bf16)
    return high, (v - high.astype(f32)).astype(bf16)


def column(table, i):
    lane = lax.broadcasted_iota(jnp.int32, table.shape, 1)
    return jnp.sum(jnp.where(lane == i, table, 0.0), 1, keepdims=True)


def split_kernel(*refs):
    inputs, outs, scratch, sem = refs[:6], refs[6:10], refs[10:16], refs[16]
    heads, residual, routes, weights, gains, scales = scratch
    send, keep, gain, scale = outs
    copies = [
        pltpu.make_async_copy(a.at[0] if i == 0 else a, t, sem.at[i])
        for i, (a, t) in enumerate(zip(inputs, scratch))
    ]
    for copy in copies:
        copy.start()
    for copy in copies:
        copy.wait()
    c = lax.axis_index("cuts")
    b = c & 1
    rows, width = heads.shape
    own = residual.shape[0]
    n_c = rows // own
    part = width // n_c
    at = lax.broadcasted_iota(jnp.int32, (rows, 1), 0) // own == c

    def wide(v):
        return jnp.where(at, jnp.concatenate([v] * n_c, 0), 0.0)

    for x in range(n_c // 2):
        low = pl.ds(2 * x * part, part)
        high = pl.ds((2 * x + 1) * part, part)
        v0 = heads[:, low] + wide(residual[:, low].astype(f32))
        v1 = heads[:, high] + wide(residual[:, high].astype(f32))
        to = pl.ds(x * part, part)
        keep[:, to] = jnp.where(b == 0, v0, v1)
        send[:, to] = jnp.where(b == 0, v1, v0)
    lane = lax.broadcasted_iota(jnp.int32, (own, PAD), 1)
    share = jnp.zeros((own, PAD), f32)
    for k in range(routes.shape[1]):
        share = share + jnp.where(lane == routes[:, k : k + 1], weights[:, k : k + 1], 0.0)
    share = wide(share)
    end = pl.ds(n_c // 2 * part, PAD)
    keep[:, end] = share
    send[:, end] = share
    scale[...] = scales[...]
    lines = part // PAD
    for i in range(lines):
        gain[:, i * PAD : (i + 1) * PAD] = gains[pl.ds(c * lines + i, 1), :]


def share_parts(v):
    high, low = halves(v)
    lane = lax.broadcasted_iota(jnp.int32, v.shape, 1)
    low = pltpu.roll(jnp.where(lane < EXPERTS, low.astype(f32), 0.0), EXPERTS, 1)
    return (jnp.where(lane < EXPERTS, high.astype(f32), 0.0) + low).astype(bf16)


def share_sum(t):
    t = t.astype(f32)
    lane = lax.broadcasted_iota(jnp.int32, t.shape, 1)
    return jnp.where(lane < EXPERTS, t + pltpu.roll(t, PAD - EXPERTS, 1), 0.0)


def join_kernel(keep, got, send, left):
    h = lax.axis_index("cuts") >> 1
    part = left.shape[1] - PAD
    v0 = keep[:, :part] + got[:, :part]
    v1 = keep[:, part : 2 * part] + got[:, part : 2 * part]
    share = keep[:, 2 * part :] + got[:, 2 * part :]
    left[:, :part] = jnp.where(h == 0, v0, v1)
    send[:, :part] = jnp.where(h == 0, v1, v0).astype(bf16)
    left[:, part:] = share
    send[:, part:] = share_parts(share)


def stream_kernel(left, got, out):
    part = left.shape[1] - PAD
    out[:, :part] = (left[:, :part] + got[:, :part].astype(f32)).astype(bf16)
    out[:, part:] = share_parts(left[:, part:] + share_sum(got[:, part:]))


def expert_of(pair, other):
    b = lax.axis_index("cuts") & 1
    return 2 * pair + (1 - b if other else b)


PIECES = ((0, True), (0, False), (1, True), (1, False))


def load_kernel(w_up, after, w_gate, *refs):
    gates, ups, sem = refs[:3], refs[3:7], refs[7]
    copies = []
    for w, outs, split in ((w_gate, gates, SPLIT), (w_up, ups, 1)):
        for out, piece in zip(outs, PIECES):
            at = pl.ds(pl.multiple_of(expert_of(*piece) * FH, FH), FH)
            step = w.shape[0] // split
            for p in range(split):
                rows = pl.ds(p * step, step)
                n = len(copies)
                copies.append(pltpu.make_async_copy(w.at[rows, at], out.at[rows], sem.at[n]))
    for copy in copies:
        copy.start()
    for copy in copies:
        copy.wait()


def load_down_kernel(after, w_down, *refs):
    outs, token, sem = refs[:-2], refs[-2], refs[-1]
    copies = []
    for i, (pair, other) in enumerate(((0, False), (0, True), (1, False), (1, True))):
        at = pl.ds(pl.multiple_of(expert_of(pair, other) * FH, FH), FH)
        copies.append(pltpu.make_async_copy(w_down.at[at], outs[i], sem.at[i]))
    for copy in copies:
        copy.start()
    for copy in copies:
        copy.wait()
    token[...] = jnp.zeros_like(token)


def expert_product(x, w_gate, w_up, out):
    tile = 256
    for w, base in ((w_gate, 0), (w_up, FH)):
        for i in range(FH // tile):
            p = jnp.dot(x[...], w[:, i * tile : (i + 1) * tile], preferred_element_type=f32)
            out[:, pl.ds(base + i * tile, tile)] = p.astype(out.dtype)


def first_kernel(s0, s1, s2, s3, gain, w_gate, w_up, x, send, share, square):
    part = x.shape[1]
    rows_e = s0.shape[0]
    weight = gain[...]
    for k, s in enumerate((s0, s1, s2, s3)):
        v = s[:, :part].astype(f32)
        at = pl.ds(k * rows_e, rows_e)
        x[at, :] = (v * weight).astype(bf16)
        square[at, :] = jnp.broadcast_to(jnp.sum(v * v, 1, keepdims=True), (rows_e, PAD))
        share[at, :] = share_sum(s[:, part:])
    expert_product(x, w_gate, w_up, send)
    send[:, 2 * FH :] = parts(square[...])


def parts(v):
    high, low = halves(v)
    lane = lax.broadcasted_iota(jnp.int32, v.shape, 1)
    return jnp.where(lane == 0, high.astype(f32), low.astype(f32)).astype(bf16)


def pair_sum(t):
    lane = lax.broadcasted_iota(jnp.int32, t.shape, 1)
    return jnp.broadcast_to(jnp.sum(jnp.where(lane < 2, t, 0.0), 1, keepdims=True), t.shape)


def product_kernel(x, w_gate, w_up, out):
    expert_product(x, w_gate, w_up, out)


def product_stream_kernel(x, up, gate_hbm, out, gate, sem):
    at = pl.ds(pl.multiple_of(expert_of(1, False) * FH, FH), FH)
    step = 256
    copies = []
    for p in range(x.shape[1] // step):
        rows = pl.ds(p * step, step)
        copies.append(pltpu.make_async_copy(gate_hbm.at[rows, at], gate.at[rows], sem.at[p]))
    for copy in copies:
        copy.start()
    for i in range(FH // step):
        to = pl.ds(i * step, step)
        out[:, pl.ds(FH + i * step, step)] = jnp.dot(x[...], up[:, to], preferred_element_type=f32)
    for p, copy in enumerate(copies):
        rows = pl.ds(p * step, step)
        copy.wait()
        v = jnp.dot(x[:, rows], gate[rows, :], preferred_element_type=f32)
        out[:, :FH] = v if p == 0 else out[:, :FH] + v


def own_expert(pair):
    e = lax.axis_index("expert")
    return e * (EXPERTS // lax.axis_size("expert")) + expert_of(pair, False)


def places(share, own_rows, slots):
    rows = share.shape[0]
    on = jnp.where(share != 0.0, 1.0, 0.0)
    row = lax.broadcasted_iota(jnp.int32, (rows, 1), 0)
    within = row % own_rows
    before = jnp.zeros_like(on)
    wide = jnp.broadcast_to(on, (rows, PAD))
    for d in range(1, own_rows):
        before = before + jnp.where(within >= d, pltpu.roll(wide, d, 0)[:, :1], 0.0)
    slot = row // own_rows * MOST + before.astype(jnp.int32)
    at = lax.broadcasted_iota(jnp.int32, (rows, slots), 1)
    return jnp.where((at == slot) & (on != 0.0), 1.0, 0.0).astype(bf16)


def packed(v, where):
    dims = (((0,), (0,)), ((), ()))
    return lax.dot_general(where, v, dims, preferred_element_type=f32).astype(bf16)


def payload(v, share, pair, own_rows, send, place):
    where = places(column(share[...], own_expert(pair)), own_rows, send.shape[0])
    place[...] = where
    send[:, : 2 * FH] = packed(v.astype(bf16), where)


def lanes(shape):
    lane = lax.broadcasted_iota(jnp.int32, shape, 1)
    row = lax.broadcasted_iota(jnp.int32, shape, 0)
    return lane == row, lane == row + shape[0]


def first_sum_kernel(own_rows, keep, got, square, share, total, send, square_out, place):
    v = keep[...] + got[:, : 2 * FH].astype(f32)
    total[...] = v
    payload(v, share, 0, own_rows, send, place)
    s = square[...] + pair_sum(got[:, 2 * FH :].astype(f32))
    square_out[...] = s
    high, low = halves(s)
    at_high, at_low = lanes(s.shape)
    t = jnp.where(at_high, high.astype(f32), jnp.where(at_low, low.astype(f32), 0.0))
    t = jnp.broadcast_to(jnp.sum(t, 0, keepdims=True), (send.shape[0], PAD))
    send[:, 2 * FH :] = t.astype(bf16)


def sum_kernel(own_rows, keep, got, share, total, send, place):
    v = keep[...] + got[...].astype(f32)
    total[...] = v
    payload(v, share, 1, own_rows, send, place)


def hidden_kernel(pair, width, total, got, first, square, place, share, scale, after, out):
    at_high, at_low = lanes(square.shape)
    t = jnp.broadcast_to(first[:16, 2 * FH :].astype(f32)[:1], square.shape)
    squares = square[:, :1] + jnp.sum(jnp.where(at_high | at_low, t, 0.0), 1, keepdims=True)
    factor = lax.rsqrt(squares / width + 1e-06)
    expert = own_expert(pair)
    coefficient = column(share[...], expert) * column(scale[...], expert)
    v = jnp.dot(place[...], got[:, : 2 * FH], preferred_element_type=f32)
    v = (total[...] + v) * factor
    g, u = v[:, :FH], v[:, FH:]
    out[...] = (g / (1.0 + jnp.exp(-g)) * u * coefficient).astype(bf16)


def down_kernel(last, *refs):
    if last:
        hidden, w_down, before, o0, o1, o2, o3 = refs
    elif len(refs) == 4:
        hidden, w_down, before, out = refs
    else:
        (hidden, w_down, out), before = refs, None
    tile = 256
    for i in range(w_down.shape[1] // tile):
        cols = pl.ds(i * tile, tile)
        p = jnp.dot(hidden[...], w_down[:, cols], preferred_element_type=f32)
        if before is not None:
            p = p + before[:, cols]
        if last:
            r = o0.shape[0]
            for k, o in enumerate((o0, o1, o2, o3)):
                o[:, cols] = p[k * r : (k + 1) * r].astype(o.dtype)
        else:
            out[:, cols] = p


def mixed_kernel(stream, own, r3, r2, r1, m0, m1, m2, m3):
    c = lax.axis_index("cuts")
    part = own.shape[1]
    v = stream[:, :part].astype(f32) + own[...]
    for r in (r1, r2, r3):
        v = v + r[...].astype(f32)
    n = m0.shape[0]
    blocks = [v[k * n : (k + 1) * n] for k in range(4)]
    for k, m in enumerate((m0, m1, m2, m3)):
        to = c ^ k
        t = jnp.where(to < 2, jnp.where(to == 0, blocks[0], blocks[1]),
                      jnp.where(to == 2, blocks[2], blocks[3]))
        m[...] = t.astype(bf16)


def final_kernel(m0, m3, m2, m1, out):
    c = lax.axis_index("cuts")
    part = m0.shape[1]
    p = [m[...].astype(f32) for m in (m0, m1, m2, m3)]
    for s in range(4):
        k = c ^ s
        t = jnp.where(k < 2, jnp.where(k == 0, p[0], p[1]), jnp.where(k == 2, p[2], p[3]))
        out[:, s * part : (s + 1) * part] = t.astype(bf16)


def fast_body(
    residual, head_partials, norm_gain, routes, route_weights, w_gate, w_up, w_down, expert_scale
):
    own_rows, width = residual.shape
    rows_e = 4 * own_rows
    part = width // 4
    rows = 4 * rows_e
    slots = rows // own_rows * MOST
    weight = pltpu.VMEM((part, FH), bf16)

    cut = (rows_e, 2 * part + PAD)
    gains, scales = norm_gain.reshape(width // PAD, PAD), expert_scale.reshape(1, EXPERTS)
    send, keep, gain, scale = call(
        split_kernel, [(cut, f32)] * 2 + [((1, part), f32), ((1, EXPERTS), f32)],
        head_partials, residual, routes, route_weights, gains, scales,
        far=6, limit=62, inside=True,
        scratch=[
            pltpu.VMEM((rows_e, width), f32), pltpu.VMEM(residual.shape, bf16),
            pltpu.VMEM(routes.shape, jnp.int32), pltpu.VMEM(route_weights.shape, f32),
            pltpu.VMEM(gains.shape, f32), pltpu.VMEM(scales.shape, f32),
            pltpu.SemaphoreType.DMA((6,)),
        ],
    )
    cut = (rows_e, part + PAD)
    send, left = call(join_kernel, [(cut, bf16), (cut, f32)], keep, swap(send, "cuts", 1), cost=COVER)
    got = swap(send, "cuts", 2)
    (s0,) = call(stream_kernel, [(cut, bf16)], left, got, cost=COVER // 4)
    s3, s2, s1 = [swap(s0, "expert", k) for k in (3, 2, 1)]
    ga0, gb0, ga1, ua0, ub0, ua1, ub1 = call(
        load_kernel, [weight] * 7, w_up, s0, w_gate, far=2, limit=4,
        scratch=[pltpu.SemaphoreType.DMA((3 * SPLIT + 4,))],
    )
    x, send, share, square = call(
        first_kernel,
        [((rows, part), bf16), ((rows, 2 * FH + PAD), bf16), ((rows, PAD), f32), ((rows, PAD), f32)],
        s0, s1, s2, s3, gain, ga0, ua0,
    )
    got = swap(send, "cuts", 1)
    full = ((rows, 2 * FH), f32)
    (keep,) = call(product_kernel, [full], x, gb0, ub0)
    table = ((rows, PAD), f32)
    sent_all = ((rows, 2 * FH), bf16)
    place = ((rows, slots), bf16)
    sent = ((slots, 2 * FH + PAD), bf16)
    total0, send, square, place0 = call(
        functools.partial(first_sum_kernel, own_rows),
        [full, sent, table, place], keep, got, square, share,
    )
    got0 = swap(send, "cuts", 2)
    (send,) = call(product_kernel, [sent_all], x, ga1, ua1)
    got = swap(send, "cuts", 1)
    (keep,) = call(
        product_stream_kernel, [full], x, ub1, w_gate, far=1, limit=47,
        scratch=[pltpu.VMEM((part, FH), bf16), pltpu.SemaphoreType.DMA((part // 256,))],
    )
    total1, send, place1 = call(
        functools.partial(sum_kernel, own_rows), [full, ((slots, 2 * FH), bf16), place], keep, got, share
    )
    got1 = swap(send, "cuts", 2)
    d0, d1, d2, d3, after = pl.pallas_call(
        load_down_kernel,
        in_specs=[HB] * 2,
        out_specs=[VM] * 5,
        out_shape=[pltpu.VMEM((FH, part), bf16)] * 4 + [jax.ShapeDtypeStruct((8, PAD), f32)],
        scratch_shapes=[pltpu.SemaphoreType.DMA((4,))],
        cost_estimate=pl.CostEstimate(flops=1, bytes_accessed=1, transcendentals=0),
        compiler_params=pltpu.CompilerParams(vmem_limit_bytes=34 * MIB),
    )(send, w_down)

    half = ((rows, FH), bf16)
    out = ((rows, part), f32)
    (h0,) = call(
        functools.partial(hidden_kernel, 0, width), [half],
        total0, got0, got0, square, place0, share, scale, after,
    )
    g0 = swap(h0, "cuts", 1)
    (t,) = call(functools.partial(down_kernel, False), [out], h0, d0)
    (h1,) = call(
        functools.partial(hidden_kernel, 1, width), [half],
        total1, got1, got0, square, place1, share, scale, t, far=1,
    )
    (t,) = call(functools.partial(down_kernel, False), [out], g0, d1, t)
    g1 = swap(h1, "cuts", 1)
    (t,) = call(functools.partial(down_kernel, False), [out], h1, d2, t)
    o0, o1, o2, o3 = call(
        functools.partial(down_kernel, True),
        [((rows_e, part), f32)] + [((rows_e, part), bf16)] * 3,
        g1, d3, t,
    )
    r3, r2, r1 = [swap(o, "expert", k) for k, o in ((3, o3), (2, o2), (1, o1))]
    m0, m1, m2, m3 = call(mixed_kernel, [((own_rows, part), bf16)] * 4, s0, o0, r3, r2, r1)
    m3, m2, m1 = [swap(m, "cuts", k) for k, m in ((3, m3), (2, m2), (1, m1))]
    (mixed,) = call(final_kernel, [((own_rows, width), bf16)], m0, m3, m2, m1)
    return mixed


def solution(mesh):
    in_specs = (
        P(("group", "expert", "cuts"), None),
        P("cuts", ("group", "expert"), None),
        P(),
        P(("group", "expert", "cuts"), None),
        P(("group", "expert", "cuts"), None),
        P("cuts", "expert"),
        P("cuts", "expert"),
        P("expert", "cuts"),
        P(),
    )
    out_specs = P(("group", "expert", "cuts"), None)
    small = mesh.shape["expert"] == 4 and mesh.shape["cuts"] == 4

    def pick_body(*args):
        fits = small and 32 * args[0].shape[0] <= PAD
        return (fast_body if fits else body)(*args)

    return jax.shard_map(
        pick_body, mesh=mesh, in_specs=in_specs, out_specs=out_specs, check_vma=False
    )
```
